512 devices in a mesh: shot: 32 (over y, z_lo), depth: 16 (over z_hi, x, core).
Axes of the slice: x: 4, y: 8, z: 8 (z_hi: 2, z_lo: 4; z = z_hi * 4 + z_lo), core: 2. Of those that a mesh axis runs over, the one named last changes fastest.
Arguments:
- courant_sq: float32 [128, 64, 128], P('depth'), may hold values from 0.03 to 0.245
- momentum: float32 [128, 64, 128], P('depth'), may hold values from -6 to 6
- fwd_prev: float32 [64, 128, 64, 128], P('shot', 'depth'), may hold values from -6 to 6
- fwd_cur: float32 [64, 128, 64, 128], P('shot', 'depth'), may hold values from -6 to 6
- adj_next: float32 [64, 128, 64, 128], P('shot', 'depth'), may hold values from -6 to 6
- adj_cur: float32 [64, 128, 64, 128], P('shot', 'depth'), may hold values from -6 to 6
- observed: float32 [64, 8, 512], P('shot'), may hold values from -24 to 24
- src_cells: int32 [64], P('shot'), may hold values from 0 to 1048575
- rec_cells: int32 [64, 512], P('shot'), may hold values from 0 to 1048575
- ckpt_step: int32 [], replicated, may hold values from 0 to 999999
Outputs:
- momentum_half: float32 [128, 64, 128], P('depth')
- kinetic: float32 [], replicated
The draws below stay inside these ranges and needn't reach their ends.
Inputs may be any that keep to these rules, and one draw needn't show every extreme that they name: `src_cells`: cell indices as defined in the reference program. `rec_cells`: cell indices as defined in the reference program.
All inputs are finite; a program needn't handle non-finite values.
Results may differ from the reference program's by a relative error of at most 0.0003.
Values sent between devices are 32-bit elements; how exact they have to be, the bound alone decides.
A program may use at most 64 MiB of HBM per device.

```python
import math
import jax
import jax.numpy as jnp
from jax import lax

NX = 64
NY = 128
STEPS = 8
NREC = 512
NZ = 128
SHOTS = 64


def draw_courant_sq(key, part):
    key = jax.random.fold_in(key, 11)
    shape = (NZ, NX, NY)
    unit = jax.random.uniform(key, shape, jnp.float32)
    return jnp.exp(math.log(0.03) + unit * (math.log(0.24) - math.log(0.03)))


def place_ends(entries, rng, least, high):
    index_at = [jax.random.randint(jax.random.fold_in(rng, axis), (), 0, length) for axis, length in enumerate(entries.shape)]
    longest = entries.shape.index(max(entries.shape))
    beside = index_at[:longest] + [(index_at[longest] + 1) % entries.shape[longest]] + index_at[longest + 1:]
    return entries.at[tuple(index_at)].set(least).at[tuple(beside)].set(high)


def level_of(rng, dims, pieces, least, high):
    loudness, own = 1.0, jax.random.fold_in(rng, 6)
    for position, blocks in pieces:
        steps = jnp.exp(jax.random.uniform(jax.random.fold_in(own, position), (blocks,), jnp.float32, least / len(pieces), high / len(pieces)))
        loudness = loudness * jnp.repeat(steps, dims[position] // blocks).reshape([-1 if axis == position else 1 for axis in range(len(dims))])
    return loudness


def noise(own_key, dims, deviation, most, split=(), held_as=jnp.bfloat16):
    array = deviation * jax.random.normal(own_key, dims, jnp.float32)
    if split:
        array = array * level_of(own_key, dims, split, -0.22, 0.18)
    return jnp.clip(array, -most, most).astype(held_as)


def setup_inputs(seed: int = 0) -> dict:
    key_of = jax.random.split(jax.random.key(seed), 11)
    courant_sq = draw_courant_sq(jax.random.fold_in(key_of[10], 71), 0)
    momentum = noise(key_of[1], (NZ, NX, NY), 1.0, 6.0, ((0, 16),), jnp.float32)
    fwd_prev = noise(key_of[2], (SHOTS, NZ, NX, NY), 1.0, 6.0, ((0, 32), (1, 16)), jnp.float32)
    fwd_cur = noise(key_of[3], (SHOTS, NZ, NX, NY), 1.0, 6.0, ((0, 32), (1, 16)), jnp.float32)
    adj_next = noise(key_of[4], (SHOTS, NZ, NX, NY), 1.0, 6.0, ((0, 32), (1, 16)), jnp.float32)
    adj_cur = noise(key_of[5], (SHOTS, NZ, NX, NY), 1.0, 6.0, ((0, 32), (1, 16)), jnp.float32)
    observed = noise(key_of[6], (SHOTS, STEPS, NREC), 4.0, 24.0, ((0, 32),), jnp.float32)
    src_cells = place_ends(jax.random.randint(key_of[7], (SHOTS,), 0, NZ * NX * NY), jax.random.fold_in(key_of[7], 1), 0, (NZ * NX * NY) - 1).astype(jnp.int32)
    rec_cells = place_ends(jax.random.randint(key_of[8], (SHOTS, NREC), 0, NZ * NX * NY), jax.random.fold_in(key_of[8], 1), 0, (NZ * NX * NY) - 1).astype(jnp.int32)
    ckpt_step = jax.random.randint(key_of[9], (), 0, 1000000).astype(jnp.int32)
    return dict(courant_sq=courant_sq, momentum=momentum, fwd_prev=fwd_prev, fwd_cur=fwd_cur, adj_next=adj_next, adj_cur=adj_cur, observed=observed, src_cells=src_cells, rec_cells=rec_cells, ckpt_step=ckpt_step)


CENTER = -2.5
NEAR = 4.0 / 3.0
FAR = -1.0 / 12.0
AMPLITUDE = 100.0
EPSILON = 1e-06

def laplace(padded):
    lateral = jnp.pad(padded[:, 2:-2], ((0, 0), (0, 0), (2, 2), (2, 2)))
    center = padded[:, 2:-2]
    along_z = NEAR * (padded[:, 1:-3] + padded[:, 3:-1]) + FAR * (padded[:, :-4] + padded[:, 4:])
    along_x = NEAR * (lateral[:, :, 1:-3, 2:-2] + lateral[:, :, 3:-1, 2:-2]) + FAR * (lateral[:, :, :-4, 2:-2] + lateral[:, :, 4:, 2:-2])
    along_y = NEAR * (lateral[:, :, 2:-2, 1:-3] + lateral[:, :, 2:-2, 3:-1]) + FAR * (lateral[:, :, 2:-2, :-4] + lateral[:, :, 2:-2, 4:])
    return 3.0 * CENTER * center + along_z + along_x + along_y

def locate(field, cell_ids, first_plane):
    shot_count, planes, rows_x, rows_y = field.shape
    plane_cells = rows_x * rows_y
    local_index = cell_ids - first_plane * plane_cells
    inside = (local_index >= 0) & (local_index < planes * plane_cells)
    target = jnp.where(inside, local_index, 0).astype(jnp.int32)
    return (inside, target)

def inject(field, cell_ids, values, first_plane):
    shot_count = field.shape[0]
    inside, target = locate(field, cell_ids, first_plane)
    amount = jnp.where(inside, values, jnp.zeros_like(values))
    flattened = field.reshape(shot_count, -1)
    lanes = jnp.arange(shot_count)[:, None]
    flattened = flattened.at[lanes, target].add(amount)
    return flattened.reshape(field.shape)

def sample(field, cell_ids, first_plane):
    shot_count = field.shape[0]
    inside, target = locate(field, cell_ids, first_plane)
    values = jnp.take_along_axis(field.reshape(shot_count, -1), target, axis=1)
    return jnp.where(inside, values, jnp.zeros_like(values))

def wave_value(start, step):
    cycle = jnp.mod(start.astype(jnp.int32) + jnp.int32(step), jnp.int32(48))
    phase = (cycle.astype(jnp.float32) - 24.0) / 12.0
    return AMPLITUDE * (1.0 - 2.0 * phase * phase) * jnp.exp(-phase * phase)

def depth_pad(field):
    return jnp.pad(field, ((0, 0), (2, 2), (0, 0), (0, 0)))

def reference(courant_sq, momentum, fwd_prev, fwd_cur, adj_next, adj_cur, observed, src_cells, rec_cells, ckpt_step):

    def one_shot(grand_total, per_shot):
        older, current, adj_later, adj_now, traces, source, receivers = per_shot
        older = older[None]
        current = current[None]
        adj_later = adj_later[None]
        adj_now = adj_now[None]
        source = source.reshape(1, 1)
        receivers = receivers[None]
        laplacians = []
        misfits = []
        for step in range(STEPS):
            laplacian = laplace(depth_pad(current))
            strength = jnp.full((1, 1), wave_value(ckpt_step, step), jnp.float32)
            laplacian = inject(laplacian, source, strength, 0)
            newer = 2.0 * current - older + courant_sq * laplacian
            misfits.append(sample(newer, receivers, 0) - traces[None, step])
            laplacians.append(laplacian)
            older, current = (current, newer)
        for step in reversed(range(STEPS)):
            adj_new = 2.0 * adj_now - adj_later + laplace(depth_pad(courant_sq * adj_now))
            adj_new = inject(adj_new, receivers, misfits[step], 0)
            grand_total = grand_total + lax.optimization_barrier(jnp.sum(adj_new * laplacians[step], axis=0))
            adj_later, adj_now = (adj_now, adj_new)
        return (grand_total, None)
    start_total = jnp.zeros((NZ, NX, NY), jnp.float32)
    gradient, _ = lax.scan(one_shot, start_total, (fwd_prev, fwd_cur, adj_next, adj_cur, observed, src_cells, rec_cells))
    depths = jnp.arange(NZ).astype(jnp.float32)
    weight = (1.0 + 2.0 * depths / (NZ - 1))[:, None, None]
    scaled = weight * gradient
    inv_scale = lax.rsqrt(jnp.mean(scaled * scaled) + EPSILON)
    momentum_half = momentum - 0.5 * inv_scale * scaled
    kinetic = 0.5 * jnp.mean(weight * momentum_half * momentum_half)
    return (momentum_half, kinetic)
```

```python
import jax
import jax.numpy as jnp
from jax import lax
from jax.experimental import pallas as pl
from jax.experimental.pallas import tpu as pltpu
from jax.sharding import PartitionSpec as P

MESH = pl.DeviceIdType.MESH
CENTER = -2.5
NEAR = 4.0 / 3.0
FAR = -1.0 / 12.0
AMPLITUDE = 100.0
EPSILON = 1e-06

SHOTS = 2
PLANES = 8
ROWS = 64
LANES = 128
STEPS = 8
HALO = 4
PAD = 8
EXT = PLANES + 4
NREC = 512


def window_kernel(
    c_in, fprev, fcur, anext, acur, observed, src, rec, ckpt,
    grad_out,
    u, p, lap, obs, cnt, hot, cs, grad, wave, stage_next, stage_cur,
    local_sem, send_sem, recv_sem, init_send, init_recv,
):
    s = lax.axis_index("shot")
    d = lax.axis_index("depth")
    size = lax.axis_size("depth")
    odd = lax.rem(d, 2)
    early_side, late_side = 1 - odd, odd
    early_id = (s, d + 1 - 2 * odd)
    has_late = ((odd == 1) & (d < size - 1)) | ((odd == 0) & (d > 0))
    late_id = (s, jnp.clip(d - 1 + 2 * odd, 0, size - 1))

    barrier = pltpu.get_barrier_semaphore()
    pl.semaphore_signal(barrier, inc=1, device_id=early_id, device_id_type=MESH)

    @pl.when(has_late)
    def _():
        pl.semaphore_signal(barrier, inc=1, device_id=late_id, device_id_type=MESH)

    data = pl.ds(PAD, ROWS)
    own = pl.ds(HALO, PLANES)
    loads = [
        pltpu.make_async_copy(fcur, u.at[1, :, own, data, :], local_sem.at[0]),
        pltpu.make_async_copy(fprev, u.at[0, :, own, data, :], local_sem.at[1]),
        pltpu.make_async_copy(c_in, cs.at[pl.ds(2, PLANES)], local_sem.at[2]),
        pltpu.make_async_copy(acur, stage_cur, local_sem.at[3]),
        pltpu.make_async_copy(anext, stage_next, local_sem.at[4]),
    ]
    for copy in loads:
        copy.start()

    pl.semaphore_wait(barrier, jnp.where(has_late, 2, 1))

    def first_copies(side, target):
        other = 1 - side
        out = []
        for width, source, slot, level in ((4, fcur, 0, 1), (2, fprev, 1, 0)):
            for shot in range(SHOTS):
                out.append(
                    pltpu.make_async_remote_copy(
                        source.at[shot, pl.ds((PLANES - width) * side, width)],
                        u.at[level, shot, pl.ds(HALO - width + (PLANES + width) * other, width), data, :],
                        init_send.at[slot, shot, side],
                        init_recv.at[slot, shot, other],
                        device_id=target,
                        device_id_type=MESH,
                    )
                )
        out.append(
            pltpu.make_async_remote_copy(
                c_in.at[pl.ds((PLANES - 2) * side, 2)],
                cs.at[pl.ds((PLANES + 2) * other, 2)],
                init_send.at[2, 0, side],
                init_recv.at[2, 0, other],
                device_id=target,
                device_id_type=MESH,
            )
        )
        return out

    def adj_copies(side, target):
        other = 1 - side
        return [
            pltpu.make_async_remote_copy(
                p.at[8, shot, pl.ds(HALO + (PLANES - 2) * side, 2), data, :],
                p.at[8, shot, pl.ds(HALO - 2 + (PLANES + 2) * other, 2), data, :],
                init_send.at[3, shot, side],
                init_recv.at[3, shot, other],
                device_id=target,
                device_id_type=MESH,
            )
            for shot in range(SHOTS)
        ]

    def halo_copy(buf, level, slot, shot, side, width, target):
        other = 1 - side
        return pltpu.make_async_remote_copy(
            buf.at[level, shot, pl.ds(HALO + (PLANES - width) * side, width), data, :],
            buf.at[level, shot, pl.ds(HALO - width + (PLANES + width) * other, width), data, :],
            send_sem.at[slot, shot, side],
            recv_sem.at[slot, shot, other],
            device_id=target,
            device_id_type=MESH,
        )

    @pl.when(has_late)
    def _():
        for copy in first_copies(late_side, late_id):
            copy.start()

    for copy in first_copies(early_side, early_id):
        copy.start()

    loads[2].wait()
    loads[3].wait()
    loads[4].wait()

    def scale(i, carry):
        factor = cs[2 + i]
        for shot in range(SHOTS):
            p[9, shot, HALO + i, PAD : PAD + ROWS, :] = factor * stage_next[shot, i]
            p[8, shot, HALO + i, PAD : PAD + ROWS, :] = factor * stage_cur[shot, i]
        return carry

    lax.fori_loop(0, PLANES, scale, 0)

    @pl.when(has_late)
    def _():
        for copy in adj_copies(late_side, late_id):
            copy.start()

    for copy in adj_copies(early_side, early_id):
        copy.start()

    def clear_pads(i, carry):
        level, plane = i // (PLANES + 2 * HALO), lax.rem(i, PLANES + 2 * HALO)
        zeros = jnp.zeros((PAD, LANES), jnp.float32)
        for buf in (u, p):
            for shot in range(SHOTS):
                buf[level, shot, plane, 0:PAD, :] = zeros
                buf[level, shot, plane, PAD + ROWS : 2 * PAD + ROWS, :] = zeros
        return carry

    lax.fori_loop(0, 10 * (PLANES + 2 * HALO), clear_pads, 0)

    @pl.when(jnp.logical_not(has_late))
    def _():
        first = (PLANES + HALO) * late_side

        def clear(i, carry):
            level, plane = i // HALO, first + lax.rem(i, HALO)
            zeros = jnp.zeros((ROWS, LANES), jnp.float32)
            for buf in (u, p):
                for shot in range(SHOTS):
                    buf[level, shot, plane, PAD : PAD + ROWS, :] = zeros
            return carry

        lax.fori_loop(0, 10 * HALO, clear, 0)
        for i in range(2):
            cs[(PLANES + 2) * late_side + i] = jnp.zeros((ROWS, LANES), jnp.float32)

    grad[...] = jnp.zeros_like(grad)

    for k in range(STEPS):
        cycle = lax.rem(ckpt[0] + k, 48).astype(jnp.float32)
        a = (jnp.full((1, LANES), cycle, jnp.float32) - 24.0) / 12.0
        wave[k : k + 1, :] = AMPLITUDE * (1.0 - 2.0 * a * a) * jnp.exp(-a * a)

    first_cell = (d * PLANES - 2) * (ROWS * LANES)
    rows_ext = EXT * ROWS
    row_at = lax.broadcasted_iota(jnp.int32, (rows_ext, NREC), 0)
    lane_at = lax.broadcasted_iota(jnp.int32, (LANES, NREC), 0)
    nt = (((1,), (1,)), ((), ()))

    def place(shot, carry):
        cell = rec[pl.ds(shot, 1), :] - first_cell
        row = lax.shift_right_arithmetic(cell, 7)
        lane = lax.bitwise_and(cell, 127)
        at_row = jnp.where(row_at == row, 1.0, 0.0).astype(jnp.bfloat16)
        lane_hit = lane_at == lane

        def put(values):
            right = jnp.where(lane_hit, values, 0.0).astype(jnp.bfloat16)
            return lax.dot_general(at_row, right, nt, preferred_element_type=jnp.float32)

        cnt[shot] = put(jnp.ones((1, NREC), jnp.float32)).reshape(EXT, ROWS, LANES)
        for k in range(STEPS):
            trace = observed[shot, k : k + 1, :]
            high = trace.astype(jnp.bfloat16).astype(jnp.float32)
            total = put(high) + put(trace - high)
            obs[k, shot] = total.reshape(EXT, ROWS, LANES)
        source = src[shot] - first_cell
        inside = lax.broadcasted_iota(jnp.int32, (ROWS, LANES), 0) * LANES + lax.broadcasted_iota(jnp.int32, (ROWS, LANES), 1)
        for plane in range(EXT):
            hot[shot, plane] = jnp.where(inside == source - plane * (ROWS * LANES), 1.0, 0.0)
        return carry

    lax.fori_loop(0, SHOTS, place, 0)

    lane_iota = lax.broadcasted_iota(jnp.int32, (ROWS, LANES), 1)
    masks = {j: (lane_iota >= j) if j > 0 else (lane_iota < LANES + j) for j in (1, 2, -1, -2)}

    def laplace(buf, level, shot, plane):
        def at(dz, dx):
            return buf[level, shot, plane + dz, PAD + dx : PAD + dx + ROWS, :]

        center = at(0, 0)

        def along_y(j):
            return jnp.where(masks[j], pltpu.roll(center, j % LANES, 1), 0.0)

        near = (at(-1, 0) + at(1, 0)) + (at(0, -1) + at(0, 1)) + (along_y(1) + along_y(-1))
        far = (at(-2, 0) + at(2, 0)) + (at(0, -2) + at(0, 2)) + (along_y(2) + along_y(-2))
        return center, 3.0 * CENTER * center + NEAR * near + FAR * far

    def forward(k, shot, start, count):
        strength = wave[pl.ds(k, 1), :]

        def one(i, carry):
            plane = start + i
            center, value = laplace(u, k + 1, shot, plane)
            value = value + strength * hot[shot, plane - 2]
            lap[k, shot, plane - 2] = value
            older = u[k, shot, plane, PAD : PAD + ROWS, :]
            u[k + 2, shot, plane, PAD : PAD + ROWS, :] = 2.0 * center - older + cs[plane - 2] * value
            return carry

        lax.fori_loop(0, count, one, 0)

    def backward(k, shot, start, count):
        def one(i, carry):
            plane = start + i
            center, value = laplace(p, k + 1, shot, plane)
            ahead = u[k + 2, shot, plane, PAD : PAD + ROWS, :]
            value = value + (cnt[shot, plane - 2] * ahead - obs[k, shot, plane - 2])
            later = p[k + 2, shot, plane, PAD : PAD + ROWS, :]
            newer = 2.0 * center - later + cs[plane - 2] * value
            p[k, shot, plane, PAD : PAD + ROWS, :] = newer
            grad[plane - 2] += newer * lap[k, shot, plane - 2]
            return carry

        lax.fori_loop(0, count, one, 0)

    def when_late(action):
        pl.when(has_late)(action)

    even = 1 - odd
    loads[0].wait()
    loads[1].wait()

    def arrived(buf, level, slot, shot, side, width, target):
        halo_copy(buf, level, slot, shot, 1 - side, width, target).wait_recv()

    def first_arrived(shot, side, target):
        copies = first_copies(1 - side, target)
        copies[shot].wait_recv()
        copies[SHOTS + shot].wait_recv()
        if shot == 0:
            copies[2 * SHOTS].wait_recv()

    def forward_round(j, carry):
        k = 2 * j

        def arrive(shot, side, target):
            @pl.when(j == 0)
            def _():
                first_arrived(shot, side, target)

            @pl.when(j > 0)
            def _():
                arrived(u, k + 1, j, shot, side, 4, target)

        def leave(shot, side, target):
            @pl.when(j < 3)
            def _():
                halo_copy(u, k + 3, j + 1, shot, side, 4, target).start()

        for shot in range(SHOTS):
            arrive(shot, early_side, early_id)
            forward(k, shot, 2 + 4 * even, 8)
            forward(k + 1, shot, 4 + 4 * even, 4)
            leave(shot, early_side, early_id)
        for shot in range(SHOTS):
            when_late(lambda: arrive(shot, late_side, late_id))
            forward(k, shot, 2 + 8 * odd, 4)
            forward(k + 1, shot, 4 + 4 * odd, 4)
            when_late(lambda: leave(shot, late_side, late_id))
        return carry

    lax.fori_loop(0, 4, forward_round, 0)

    def adj_arrived(shot, side, target):
        adj_copies(1 - side, target)[shot].wait_recv()

    for shot in range(SHOTS):
        adj_arrived(shot, early_side, early_id)
        backward(7, shot, 4 + 2 * even, 6)
        halo_copy(p, 7, 4, shot, early_side, 4, early_id).start()
    for shot in range(SHOTS):
        when_late(lambda: adj_arrived(shot, late_side, late_id))
        backward(7, shot, 4 + 6 * odd, 2)
        when_late(lambda: halo_copy(p, 7, 4, shot, late_side, 4, late_id).start())

    def backward_round(i, carry):
        k = 6 - 2 * i

        def leave(shot, side, target):
            @pl.when(i < 2)
            def _():
                halo_copy(p, k - 1, 5 + i, shot, side, 4, target).start()

            @pl.when(i == 2)
            def _():
                halo_copy(p, k - 1, 5 + i, shot, side, 2, target).start()

        for shot in range(SHOTS):
            arrived(p, k + 1, 4 + i, shot, early_side, 4, early_id)
            backward(k, shot, 2 + 4 * even, 8)
            backward(k - 1, shot, 4 + 4 * even, 4)
            leave(shot, early_side, early_id)
        for shot in range(SHOTS):
            when_late(lambda: arrived(p, k + 1, 4 + i, shot, late_side, 4, late_id))
            backward(k, shot, 2 + 8 * odd, 4)
            backward(k - 1, shot, 4 + 4 * odd, 4)
            when_late(lambda: leave(shot, late_side, late_id))
        return carry

    lax.fori_loop(0, 3, backward_round, 0)

    for shot in range(SHOTS):
        arrived(p, 1, 7, shot, early_side, 2, early_id)
        backward(0, shot, 4 + 2 * even, 6)
    for shot in range(SHOTS):
        when_late(lambda: arrived(p, 1, 7, shot, late_side, 2, late_id))
        backward(0, shot, 4 + 6 * odd, 2)

    def finish(i, carry):
        grad_out[i] = grad[2 + i] / cs[2 + i]
        return carry

    lax.fori_loop(0, PLANES, finish, 0)

    def sent(side, target):
        for copy in first_copies(side, target) + adj_copies(side, target):
            copy.wait_send()
        for shot in range(SHOTS):
            for slot, buf, level in ((1, u, 3), (2, u, 5), (3, u, 7), (4, p, 7), (5, p, 5), (6, p, 3)):
                halo_copy(buf, level, slot, shot, side, 4, target).wait_send()
            halo_copy(p, 1, 7, shot, side, 2, target).wait_send()

    sent(early_side, early_id)
    when_late(lambda: sent(late_side, late_id))


def window(c, fprev, fcur, anext, acur, observed, src, rec, ckpt):
    any_space = pl.BlockSpec(memory_space=pl.ANY)
    in_vmem = pl.BlockSpec(memory_space=pltpu.VMEM)
    in_smem = pl.BlockSpec(memory_space=pltpu.SMEM)
    padded = (10, SHOTS, PLANES + 2 * HALO, ROWS + 2 * PAD, LANES)
    f32 = jnp.float32
    return pl.pallas_call(
        window_kernel,
        out_shape=jax.ShapeDtypeStruct((PLANES, ROWS, LANES), f32),
        in_specs=[any_space] * 5 + [in_vmem, in_smem, in_vmem, in_smem],
        out_specs=in_vmem,
        scratch_shapes=[
            pltpu.VMEM(padded, f32),
            pltpu.VMEM(padded, f32),
            pltpu.VMEM((STEPS, SHOTS, EXT, ROWS, LANES), f32),
            pltpu.VMEM((STEPS, SHOTS, EXT, ROWS, LANES), f32),
            pltpu.VMEM((SHOTS, EXT, ROWS, LANES), f32),
            pltpu.VMEM((SHOTS, EXT, ROWS, LANES), f32),
            pltpu.VMEM((EXT, ROWS, LANES), f32),
            pltpu.VMEM((EXT, ROWS, LANES), f32),
            pltpu.VMEM((STEPS, LANES), f32),
            pltpu.VMEM((SHOTS, PLANES, ROWS, LANES), f32),
            pltpu.VMEM((SHOTS, PLANES, ROWS, LANES), f32),
            pltpu.SemaphoreType.DMA((5,)),
            pltpu.SemaphoreType.DMA((8, SHOTS, 2)),
            pltpu.SemaphoreType.DMA((8, SHOTS, 2)),
            pltpu.SemaphoreType.DMA((4, SHOTS, 2)),
            pltpu.SemaphoreType.DMA((4, SHOTS, 2)),
        ],
        compiler_params=pltpu.CompilerParams(
            collective_id=0, has_side_effects=True, vmem_limit_bytes=60 * 1024 * 1024
        ),
        name="window",
    )(c, fprev, fcur, anext, acur, observed, src, rec, ckpt)


def reduce_kernel(
    grad, moment, half_out, kinetic_out,
    parts, scaled, tiles, depth_tiles,
    send_sem, recv_sem,
):
    s, d = lax.axis_index("shot"), lax.axis_index("depth")
    ns, nd = lax.axis_size("shot"), lax.axis_size("depth")
    per_plane = ns // PLANES
    cells_all = nd * PLANES * ROWS * LANES

    def shot_peers(action):
        def one(r, carry):
            action(lax.rem(s + r, ns))
            return carry

        lax.fori_loop(1, ns, one, 0)

    def depth_peers(action):
        def one(r, carry):
            action(lax.rem(d + r, nd))
            return carry

        lax.fori_loop(1, nd, one, 0)

    barrier = pltpu.get_barrier_semaphore()
    shot_peers(lambda j: pl.semaphore_signal(barrier, inc=1, device_id=(j, d), device_id_type=MESH))
    depth_peers(lambda j: pl.semaphore_signal(barrier, inc=1, device_id=(s, j), device_id_type=MESH))
    pl.semaphore_wait(barrier, ns + nd - 2)

    def remote(source, target, sem, device):
        return pltpu.make_async_remote_copy(
            source, target, send_sem.at[sem], recv_sem.at[sem], device_id=device, device_id_type=MESH
        )

    shot_peers(lambda j: remote(grad.at[j], parts.at[s], 0, (j, d)).start())
    parts[s] = grad[s]
    every = pl.ds(0, ns - 1)
    remote(parts.at[every], parts.at[every], 0, (s, d)).wait_recv()
    total = lax.fori_loop(1, ns, lambda j, t: t + parts[j], parts[0])
    plane = d * PLANES + s // per_plane
    weight = 1.0 + 2.0 * plane.astype(jnp.float32) / (nd * PLANES - 1)
    mine = weight * total
    scaled[s] = mine
    old = moment[s]
    sums = (jnp.sum(mine * mine), weight * jnp.sum(old * old), weight * jnp.sum(old * mine), weight * jnp.sum(mine * mine))
    for q, value in enumerate(sums):
        tiles[s, q : q + 1, :] = jnp.full((1, LANES), value, jnp.float32)
    tiles[s, 4:8, :] = jnp.zeros((4, LANES), jnp.float32)
    shot_peers(lambda j: remote(tiles.at[s], tiles.at[s], 1, (j, d)).start())
    shot_peers(lambda j: remote(scaled.at[s], scaled.at[s], 2, (j, d)).start())
    remote(tiles.at[every], tiles.at[every], 1, (s, d)).wait_recv()
    depth_tiles[d] = lax.fori_loop(1, ns, lambda j, t: t + tiles[j], tiles[0])
    depth_peers(lambda j: remote(depth_tiles.at[d], depth_tiles.at[d], 3, (s, j)).start())
    others = pl.ds(0, nd - 1)
    remote(depth_tiles.at[others], depth_tiles.at[others], 3, (s, d)).wait_recv()
    grand = lax.fori_loop(1, nd, lambda j, t: t + depth_tiles[j], depth_tiles[0])
    step = 0.5 * lax.rsqrt(grand[0:1, :] / cells_all + EPSILON)
    energy = grand[1:2, :] - 2.0 * step * grand[2:3, :] + step * step * grand[3:4, :]
    kinetic_out[...] = 0.5 * energy / cells_all
    remote(scaled.at[every], scaled.at[every], 2, (s, d)).wait_recv()

    def update(j, carry):
        half_out[j] = moment[j] - step * scaled[j]
        return carry

    lax.fori_loop(0, ns, update, 0)
    remote(parts.at[every], parts.at[every], 0, (s, d)).wait_send()
    remote(tiles.at[every], tiles.at[every], 1, (s, d)).wait_send()
    remote(scaled.at[every], scaled.at[every], 2, (s, d)).wait_send()
    remote(depth_tiles.at[others], depth_tiles.at[others], 3, (s, d)).wait_send()


def reduce_and_step(grad, momentum, ns, nd):
    in_vmem = pl.BlockSpec(memory_space=pltpu.VMEM)
    f32 = jnp.float32
    blocks = (ns, PLANES * ROWS // ns, LANES)
    half, kinetic = pl.pallas_call(
        reduce_kernel,
        out_shape=(jax.ShapeDtypeStruct(blocks, f32), jax.ShapeDtypeStruct((1, LANES), f32)),
        in_specs=[in_vmem] * 2,
        out_specs=(in_vmem, in_vmem),
        scratch_shapes=[
            pltpu.VMEM(blocks, f32),
            pltpu.VMEM(blocks, f32),
            pltpu.VMEM((ns, 8, LANES), f32),
            pltpu.VMEM((nd, 8, LANES), f32),
            pltpu.SemaphoreType.DMA((4,)),
            pltpu.SemaphoreType.DMA((4,)),
        ],
        compiler_params=pltpu.CompilerParams(collective_id=1, has_side_effects=True),
        name="reduce",
    )(grad.reshape(blocks), momentum.reshape(blocks))
    return half.reshape(momentum.shape), kinetic[0, 0]


def solution(mesh):
    def shards(c, momentum, fprev, fcur, anext, acur, observed, src, rec, ckpt):
        grad = window(c, fprev, fcur, anext, acur, observed, src, rec, ckpt.reshape(1))
        return reduce_and_step(grad, momentum, mesh.shape["shot"], mesh.shape["depth"])

    placed = (
        P("depth", None, None),
        P("depth", None, None),
        P("shot", "depth", None, None),
        P("shot", "depth", None, None),
        P("shot", "depth", None, None),
        P("shot", "depth", None, None),
        P("shot", None, None),
        P("shot"),
        P("shot", None),
        P(),
    )
    return jax.shard_map(
        shards, mesh=mesh, in_specs=placed, out_specs=(P("depth", None, None), P()), check_vma=False
    )
```

```python
import jax
import jax.numpy as jnp
from jax import lax
from jax.experimental import pallas as pl
from jax.experimental.pallas import tpu as pltpu
from jax.sharding import PartitionSpec as P

MESH = pl.DeviceIdType.MESH
CENTER = -2.5
NEAR = 4.0 / 3.0
FAR = -1.0 / 12.0
AMPLITUDE = 100.0
EPSILON = 1e-06

SHOTS = 2
PLANES = 8
ROWS = 64
LANES = 128
STEPS = 8
HALO = 4
PAD = 8
EXT = PLANES + 4
NREC = 512
Z_LO = 4


def window_kernel(
    c_in, fprev, fcur, anext, acur, observed, src, rec, ckpt, moment,
    half_out, kinetic_out,
    u, p, lap, obs, cnt, hot, cs, grad, wave, stage_next, stage_cur,
    blocks, parts, scaled, tiles, depth_tiles,
    relay,
    local_sem, send_sem, recv_sem, init_send, init_recv, parcel_send, parcel_recv, relay_send, relay_recv,
    all_send, all_recv, token,
):
    s = lax.axis_index("shot")
    d = lax.axis_index("depth")
    shots, size = lax.axis_size("shot"), lax.axis_size("depth")
    rows_y, half = shots // Z_LO, size // 2
    y, z_lo, x_core = s // Z_LO, lax.rem(s, Z_LO), lax.rem(d, half)
    odd = lax.rem(d, 2)
    early_side, late_side = 1 - odd, odd
    early_id = (s, d + 1 - 2 * odd)
    has_late = ((odd == 1) & (d < size - 1)) | ((odd == 0) & (d > 0))
    late_id = (s, jnp.clip(d - 1 + 2 * odd, 0, size - 1))

    def each(count, action):
        def one(r, carry):
            action(r)
            return carry

        lax.fori_loop(1, count, one, 0)

    def y_peer(r):
        return (lax.rem(y + r, rows_y) * Z_LO + z_lo, d)

    far_side = (s, lax.rem(d + half, size))
    at_cut = (d == half - 1) | (d == half)

    barrier = pltpu.get_barrier_semaphore()

    def greet(device):
        pl.semaphore_signal(barrier, inc=1, device_id=device, device_id_type=MESH)

    @pl.when(at_cut)
    def _():
        greet((s, size - 1 - d))

    greet(far_side)
    each(rows_y, lambda r: greet(y_peer(r)))
    each(Z_LO, lambda r: greet((y * Z_LO + lax.rem(z_lo + r, Z_LO), d)))
    each(half, lambda r: greet((s, d - x_core + lax.rem(x_core + r, half))))

    data = pl.ds(PAD, ROWS)
    own = pl.ds(HALO, PLANES)
    loads = [
        pltpu.make_async_copy(fcur, u.at[1, :, own, data, :], local_sem.at[0]),
        pltpu.make_async_copy(fprev, u.at[0, :, own, data, :], local_sem.at[1]),
        pltpu.make_async_copy(c_in, cs.at[pl.ds(2, PLANES)], local_sem.at[2]),
        pltpu.make_async_copy(acur, stage_cur, local_sem.at[3]),
        pltpu.make_async_copy(anext, stage_next, local_sem.at[4]),
    ]
    for copy in loads:
        copy.start()

    pl.semaphore_wait(barrier, rows_y + Z_LO + half - 2 + jnp.where(at_cut, 1, 0))

    def copy_to(source, landing, send, recv, target):
        return pltpu.make_async_remote_copy(
            source, landing, send, recv, device_id=target, device_id_type=MESH
        )

    def first_copy(shot, side, target):
        return copy_to(
            fcur.at[shot, pl.ds((PLANES - 2) * side, 2)],
            u.at[1, shot, pl.ds(HALO - 2 + (PLANES + 2) * (1 - side), 2), data, :],
            init_send.at[shot, side], init_recv.at[shot, 1 - side], target,
        )

    def parcel(i, side):
        other = 1 - side
        if i == 0:
            return c_in.at[pl.ds((PLANES - 2) * side, 2)], cs.at[pl.ds((PLANES + 2) * other, 2)], relay.at[pl.ds(0, 2)]
        level, shot = (9, i - 1) if i < 3 else (8, i - 3)
        width = 2 if i < 3 else 4
        return (
            p.at[level, shot, pl.ds(HALO + (PLANES - width) * side, width), data, :],
            p.at[level, shot, pl.ds(HALO - width + (PLANES + width) * other, width), data, :],
            relay.at[pl.ds(2 * i if i < 3 else 4 * i - 6, width)],
        )

    def parcel_copy(i, side, target):
        source, landing, _ = parcel(i, side)
        return copy_to(source, landing, parcel_send.at[i, side], parcel_recv.at[i, 1 - side], target)

    relay_id = (s, jnp.where(d < half, 0, size - 1))
    relays = (d == 0) | (d == size - 1)

    def parcel_to_relay(i, side):
        source, _, middle = parcel(i, side)
        return copy_to(source, middle, parcel_send.at[i, side], relay_recv.at[i], relay_id)

    def parcel_from_relay(i, side):
        _, landing, middle = parcel(i, side)
        return copy_to(middle, landing, relay_send.at[i], parcel_recv.at[i, 1 - side], far_side)

    def post(items):
        for i in items:
            @pl.when(at_cut)
            def _():
                parcel_to_relay(i, late_side).start()

            @pl.when(has_late & jnp.logical_not(at_cut))
            def _():
                parcel_copy(i, late_side, late_id).start()

        for i in items:
            parcel_copy(i, early_side, early_id).start()

    def when_late(action):
        pl.when(has_late)(action)

    def halo_copy(buf, level, slot, shot, side, width, target):
        other = 1 - side
        return pltpu.make_async_remote_copy(
            buf.at[level, shot, pl.ds(HALO + (PLANES - width) * side, width), data, :],
            buf.at[level, shot, pl.ds(HALO - width + (PLANES + width) * other, width), data, :],
            send_sem.at[slot, shot, side],
            recv_sem.at[slot, shot, other],
            device_id=target,
            device_id_type=MESH,
        )

    for shot in range(SHOTS):
        when_late(lambda: first_copy(shot, late_side, late_id).start())
    for shot in range(SHOTS):
        first_copy(shot, early_side, early_id).start()
    post((0,))

    def pass_on(device):
        pl.semaphore_signal(token, inc=1, device_id=device, device_id_type=MESH)

    each(rows_y, lambda r: pass_on(y_peer(r)))
    pass_on(far_side)

    loads[2].wait()
    loads[3].wait()
    loads[4].wait()

    def scale(i, carry):
        factor = cs[2 + i]
        for shot in range(SHOTS):
            p[9, shot, HALO + i, PAD : PAD + ROWS, :] = factor * stage_next[shot, i]
            p[8, shot, HALO + i, PAD : PAD + ROWS, :] = factor * stage_cur[shot, i]
        return carry

    lax.fori_loop(0, PLANES, scale, 0)

    post(range(1, 5))

    def clear_pads(i, carry):
        level, plane = i // (PLANES + 2 * HALO), lax.rem(i, PLANES + 2 * HALO)
        zeros = jnp.zeros((PAD, LANES), jnp.float32)
        for buf in (u, p):
            for shot in range(SHOTS):
                buf[level, shot, plane, 0:PAD, :] = zeros
                buf[level, shot, plane, PAD + ROWS : 2 * PAD + ROWS, :] = zeros
        return carry

    lax.fori_loop(0, 10 * (PLANES + 2 * HALO), clear_pads, 0)

    @pl.when(jnp.logical_not(has_late))
    def _():
        first = (PLANES + HALO) * late_side

        def clear(i, carry):
            level, plane = i // HALO, first + lax.rem(i, HALO)
            zeros = jnp.zeros((ROWS, LANES), jnp.float32)
            for buf in (u, p):
                for shot in range(SHOTS):
                    buf[level, shot, plane, PAD : PAD + ROWS, :] = zeros
            return carry

        lax.fori_loop(0, 10 * HALO, clear, 0)
        for i in range(2):
            cs[(PLANES + 2) * late_side + i] = jnp.zeros((ROWS, LANES), jnp.float32)

    grad[...] = jnp.zeros_like(grad)

    for k in range(STEPS):
        cycle = lax.rem(ckpt[0] + k, 48).astype(jnp.float32)
        a = (jnp.full((1, LANES), cycle, jnp.float32) - 24.0) / 12.0
        wave[k : k + 1, :] = AMPLITUDE * (1.0 - 2.0 * a * a) * jnp.exp(-a * a)

    first_cell = (d * PLANES - 2) * (ROWS * LANES)
    rows_ext = EXT * ROWS
    row_at = lax.broadcasted_iota(jnp.int32, (rows_ext, NREC), 0)
    lane_at = lax.broadcasted_iota(jnp.int32, (LANES, NREC), 0)
    nt = (((1,), (1,)), ((), ()))

    def place(shot, carry):
        cell = rec[pl.ds(shot, 1), :] - first_cell
        row = lax.shift_right_arithmetic(cell, 7)
        lane = lax.bitwise_and(cell, 127)
        at_row = jnp.where(row_at == row, 1.0, 0.0).astype(jnp.bfloat16)
        lane_hit = lane_at == lane

        def put(values):
            right = jnp.where(lane_hit, values, 0.0).astype(jnp.bfloat16)
            return lax.dot_general(at_row, right, nt, preferred_element_type=jnp.float32)

        cnt[shot] = put(jnp.ones((1, NREC), jnp.float32)).reshape(EXT, ROWS, LANES)
        for k in range(STEPS):
            trace = observed[shot, k : k + 1, :]
            high = trace.astype(jnp.bfloat16).astype(jnp.float32)
            total = put(high) + put(trace - high)
            obs[k, shot] = total.reshape(EXT, ROWS, LANES)
        source = src[shot] - first_cell
        inside = lax.broadcasted_iota(jnp.int32, (ROWS, LANES), 0) * LANES + lax.broadcasted_iota(jnp.int32, (ROWS, LANES), 1)
        for plane in range(EXT):
            hot[shot, plane] = jnp.where(inside == source - plane * (ROWS * LANES), 1.0, 0.0)
        return carry

    lax.fori_loop(0, SHOTS, place, 0)

    lane_iota = lax.broadcasted_iota(jnp.int32, (ROWS, LANES), 1)
    masks = {j: (lane_iota >= j) if j > 0 else (lane_iota < LANES + j) for j in (1, 2, -1, -2)}

    def laplaces(buf, level, shot, start, count):
        def at(plane, dx):
            return buf[level, shot, start + plane, PAD + dx : PAD + dx + ROWS, :]

        def along_y(value, j):
            return jnp.where(masks[j], pltpu.roll(value, j % LANES, 1), 0.0)

        planes = {i: at(i, 0) for i in range(-2, count + 2)}
        out = []
        for i in range(count):
            center = planes[i]
            near = (planes[i - 1] + planes[i + 1]) + (at(i, -1) + at(i, 1)) + (along_y(center, 1) + along_y(center, -1))
            far = (planes[i - 2] + planes[i + 2]) + (at(i, -2) + at(i, 2)) + (along_y(center, 2) + along_y(center, -2))
            out.append((center, 3.0 * CENTER * center + NEAR * near + FAR * far))
        return out

    def forward(k, shot, start, count):
        strength = wave[pl.ds(k, 1), :]
        done = []
        for i, (center, value) in enumerate(laplaces(u, k + 1, shot, start, count)):
            plane = start + i
            value = value + strength * hot[shot, plane - 2]
            older = u[k, shot, plane, PAD : PAD + ROWS, :]
            done.append((plane, value, 2.0 * center - older + cs[plane - 2] * value))
        for plane, value, newer in done:
            lap[k, shot, plane - 2] = value
            u[k + 2, shot, plane, PAD : PAD + ROWS, :] = newer

    def backward(k, shot, start, count):
        done = []
        for i, (center, value) in enumerate(laplaces(p, k + 1, shot, start, count)):
            plane = start + i
            ahead = u[k + 2, shot, plane, PAD : PAD + ROWS, :]
            value = value + (cnt[shot, plane - 2] * ahead - obs[k, shot, plane - 2])
            later = p[k + 2, shot, plane, PAD : PAD + ROWS, :]
            newer = 2.0 * center - later + cs[plane - 2] * value
            done.append((plane, newer, grad[plane - 2] + newer * lap[k, shot, plane - 2]))
        for plane, newer, term in done:
            p[k, shot, plane, PAD : PAD + ROWS, :] = newer
            grad[plane - 2] = term

    even = 1 - odd
    loads[0].wait()
    loads[1].wait()

    def arrived(buf, level, slot, shot, side, width, target):
        halo_copy(buf, level, slot, shot, 1 - side, width, target).wait_recv()

    for shot in range(SHOTS):
        first_copy(shot, 1 - early_side, early_id).wait_recv()
        forward(0, shot, 4 + 2 * even, 6)
        halo_copy(u, 2, 0, shot, early_side, 4, early_id).start()
    for shot in range(SHOTS):
        when_late(lambda: first_copy(shot, 1 - late_side, late_id).wait_recv())
        forward(0, shot, 4 + 6 * odd, 2)
        when_late(lambda: halo_copy(u, 2, 0, shot, late_side, 4, late_id).start())

    @pl.when(relays)
    def _():
        for i in range(5):
            parcel_to_relay(i, early_side).wait_recv()
            parcel_from_relay(i, early_side).start()

    parcel_copy(0, 1 - early_side, early_id).wait_recv()
    when_late(lambda: parcel_copy(0, 1 - late_side, late_id).wait_recv())

    def forward_round(j, carry):
        k = 2 * j + 1

        def leave(shot, side, target):
            @pl.when(j < 3)
            def _():
                halo_copy(u, k + 3, j + 1, shot, side, 4, target).start()

        def second(shot, start):
            @pl.when(j < 3)
            def _():
                forward(k + 1, shot, start, 4)

        for shot in range(SHOTS):
            arrived(u, k + 1, j, shot, early_side, 4, early_id)
            forward(k, shot, 2 + 4 * even, 8)
            second(shot, 4 + 4 * even)
            leave(shot, early_side, early_id)
        for shot in range(SHOTS):
            when_late(lambda: arrived(u, k + 1, j, shot, late_side, 4, late_id))
            forward(k, shot, 2 + 8 * odd, 4)
            second(shot, 4 + 4 * odd)
            when_late(lambda: leave(shot, late_side, late_id))
        return carry

    lax.fori_loop(0, 4, forward_round, 0)

    for i in range(1, 5):
        parcel_copy(i, 1 - early_side, early_id).wait_recv()
        when_late(lambda: parcel_copy(i, 1 - late_side, late_id).wait_recv())

    def backward_round(i, carry):
        k = 7 - 2 * i

        def arrive(shot, side, target):
            @pl.when(i > 0)
            def _():
                arrived(p, k + 1, 3 + i, shot, side, 4, target)

        def leave(shot, side, target):
            @pl.when(i < 3)
            def _():
                halo_copy(p, k - 1, 4 + i, shot, side, 4, target).start()

        for shot in range(SHOTS):
            arrive(shot, early_side, early_id)
            backward(k, shot, 2 + 4 * even, 8)
            backward(k - 1, shot, 4 + 4 * even, 4)
            leave(shot, early_side, early_id)
        for shot in range(SHOTS):
            when_late(lambda: arrive(shot, late_side, late_id))
            backward(k, shot, 2 + 8 * odd, 4)
            backward(k - 1, shot, 4 + 4 * odd, 4)
            when_late(lambda: leave(shot, late_side, late_id))
        return carry

    lax.fori_loop(0, 4, backward_round, 0)

    per_plane = shots // PLANES
    block_rows = ROWS // per_plane
    cells_all = size * PLANES * ROWS * LANES

    def cut(i, carry):
        blocks[pl.ds(i * per_plane, per_plane)] = (grad[2 + i] / cs[2 + i]).reshape(per_plane, block_rows, LANES)
        return carry

    lax.fori_loop(0, PLANES, cut, 0)

    def remote(source, target, sem, device):
        return pltpu.make_async_remote_copy(
            source, target, all_send.at[sem], all_recv.at[sem], device_id=device, device_id_type=MESH
        )

    def to_shots(source_of, target, sem):
        def one(r):
            j = lax.rem(s + r, shots)
            remote(source_of(j), target, sem, (j, d)).start()

        each(shots, one)

    others, others_depth = pl.ds(0, shots - 1), pl.ds(0, size - 1)
    pl.semaphore_wait(token, rows_y)
    to_shots(lambda j: blocks.at[j], parts.at[s], 0)
    parts[s] = blocks[s]
    remote(parts.at[others], parts.at[others], 0, (s, d)).wait_recv()
    total = lax.fori_loop(1, shots, lambda j, t: t + parts[j], parts[0])
    plane = d * PLANES + s // per_plane
    weight = 1.0 + 2.0 * plane.astype(jnp.float32) / (size * PLANES - 1)
    mine = weight * total
    scaled[s] = mine
    old = moment[s]
    squares = jnp.sum(mine * mine)
    for q, value in enumerate((squares, weight * jnp.sum(old * old), weight * jnp.sum(old * mine), weight * squares)):
        tiles[s, q : q + 1, :] = jnp.full((1, LANES), value, jnp.float32)
    tiles[s, 4:8, :] = jnp.zeros((4, LANES), jnp.float32)
    to_shots(lambda j: tiles.at[s], tiles.at[s], 1)
    to_shots(lambda j: scaled.at[s], scaled.at[s], 2)
    remote(tiles.at[others], tiles.at[others], 1, (s, d)).wait_recv()
    depth_tiles[d] = lax.fori_loop(1, shots, lambda j, t: t + tiles[j], tiles[0])

    def to_depth(r):
        j = lax.rem(d + r, size)
        remote(depth_tiles.at[d], depth_tiles.at[d], 3, (s, j)).start()

    each(size, to_depth)
    remote(depth_tiles.at[others_depth], depth_tiles.at[others_depth], 3, (s, d)).wait_recv()
    grand = lax.fori_loop(1, size, lambda j, t: t + depth_tiles[j], depth_tiles[0])
    step = 0.5 * lax.rsqrt(grand[0:1, :] / cells_all + EPSILON)
    energy = grand[1:2, :] - 2.0 * step * grand[2:3, :] + step * step * grand[3:4, :]
    kinetic_out[...] = 0.5 * energy / cells_all
    remote(scaled.at[others], scaled.at[others], 2, (s, d)).wait_recv()

    def update(j, carry):
        half_out[j] = moment[j] - step * scaled[j]
        return carry

    lax.fori_loop(0, shots, update, 0)

    def sent(side, target):
        for i in range(5):
            parcel_copy(i, side, target).wait_send()
        for shot in range(SHOTS):
            first_copy(shot, side, target).wait_send()
            for slot, buf, level in ((0, u, 2), (1, u, 4), (2, u, 6), (3, u, 8), (4, p, 6), (5, p, 4), (6, p, 2)):
                halo_copy(buf, level, slot, shot, side, 4, target).wait_send()

    sent(early_side, early_id)
    when_late(lambda: sent(late_side, late_id))

    @pl.when(relays)
    def _():
        for i in range(5):
            parcel_from_relay(i, early_side).wait_send()

    remote(parts.at[others], parts.at[others], 0, (s, d)).wait_send()
    remote(tiles.at[others], tiles.at[others], 1, (s, d)).wait_send()
    remote(scaled.at[others], scaled.at[others], 2, (s, d)).wait_send()
    remote(depth_tiles.at[others_depth], depth_tiles.at[others_depth], 3, (s, d)).wait_send()


def window(c, momentum, fprev, fcur, anext, acur, observed, src, rec, ckpt, ns, nd):
    any_space = pl.BlockSpec(memory_space=pl.ANY)
    in_vmem = pl.BlockSpec(memory_space=pltpu.VMEM)
    in_smem = pl.BlockSpec(memory_space=pltpu.SMEM)
    padded = (10, SHOTS, PLANES + 2 * HALO, ROWS + 2 * PAD, LANES)
    f32 = jnp.float32
    blocks = (ns, PLANES * ROWS // ns, LANES)
    half, kinetic = pl.pallas_call(
        window_kernel,
        out_shape=(jax.ShapeDtypeStruct(blocks, f32), jax.ShapeDtypeStruct((1, LANES), f32)),
        in_specs=[any_space] * 5 + [in_vmem, in_smem, in_vmem, in_smem, in_vmem],
        out_specs=(in_vmem, in_vmem),
        scratch_shapes=[
            pltpu.VMEM(padded, f32),
            pltpu.VMEM(padded, f32),
            pltpu.VMEM((STEPS, SHOTS, EXT, ROWS, LANES), f32),
            pltpu.VMEM((STEPS, SHOTS, EXT, ROWS, LANES), f32),
            pltpu.VMEM((SHOTS, EXT, ROWS, LANES), f32),
            pltpu.VMEM((SHOTS, EXT, ROWS, LANES), f32),
            pltpu.VMEM((EXT, ROWS, LANES), f32),
            pltpu.VMEM((EXT, ROWS, LANES), f32),
            pltpu.VMEM((STEPS, LANES), f32),
            pltpu.VMEM((SHOTS, PLANES, ROWS, LANES), f32),
            pltpu.VMEM((SHOTS, PLANES, ROWS, LANES), f32),
            pltpu.VMEM(blocks, f32),
            pltpu.VMEM(blocks, f32),
            pltpu.VMEM(blocks, f32),
            pltpu.VMEM((ns, 8, LANES), f32),
            pltpu.VMEM((nd, 8, LANES), f32),
            pltpu.VMEM((14, ROWS, LANES), f32),
            pltpu.SemaphoreType.DMA((5,)),
            pltpu.SemaphoreType.DMA((7, SHOTS, 2)),
            pltpu.SemaphoreType.DMA((7, SHOTS, 2)),
            pltpu.SemaphoreType.DMA((SHOTS, 2)),
            pltpu.SemaphoreType.DMA((SHOTS, 2)),
            pltpu.SemaphoreType.DMA((5, 2)),
            pltpu.SemaphoreType.DMA((5, 2)),
            pltpu.SemaphoreType.DMA((5,)),
            pltpu.SemaphoreType.DMA((5,)),
            pltpu.SemaphoreType.DMA((4,)),
            pltpu.SemaphoreType.DMA((4,)),
            pltpu.SemaphoreType.REGULAR,
        ],
        compiler_params=pltpu.CompilerParams(
            collective_id=0, has_side_effects=True, vmem_limit_bytes=60 * 1024 * 1024
        ),
        name="window",
    )(c, fprev, fcur, anext, acur, observed, src, rec, ckpt, momentum.reshape(blocks))
    return half.reshape(momentum.shape), kinetic[0, 0]


def solution(mesh):
    def shards(c, momentum, fprev, fcur, anext, acur, observed, src, rec, ckpt):
        return window(
            c, momentum, fprev, fcur, anext, acur, observed, src, rec, ckpt.reshape(1),
            mesh.shape["shot"], mesh.shape["depth"],
        )

    placed = (
        P("depth", None, None),
        P("depth", None, None),
        P("shot", "depth", None, None),
        P("shot", "depth", None, None),
        P("shot", "depth", None, None),
        P("shot", "depth", None, None),
        P("shot", None, None),
        P("shot"),
        P("shot", None),
        P(),
    )
    return jax.shard_map(
        shards, mesh=mesh, in_specs=placed, out_specs=(P("depth", None, None), P()), check_vma=False
    )
```

```python
import jax
import jax.numpy as jnp
from jax import lax
from jax.experimental import pallas as pl
from jax.experimental.pallas import tpu as pltpu
from jax.sharding import PartitionSpec as P

MESH = pl.DeviceIdType.MESH
CENTER = -2.5
NEAR = 4.0 / 3.0
FAR = -1.0 / 12.0
AMPLITUDE = 100.0
EPSILON = 1e-06

SHOTS = 2
PLANES = 8
ROWS = 64
LANES = 128
STEPS = 8
HALO = 4
PAD = 8
EXT = PLANES + 4
NREC = 512
Z_LO = 4


def window_kernel(
    c_in, fprev, fcur, anext, acur, observed_in, src, rec_in, ckpt, moment_in,
    half_out, kinetic_out,
    u, p, lap, obs, cnt, hot, cs, grad, wave, stage_next, stage_cur,
    blocks, parts, scaled, z_tiles, xy_tiles,
    relay, observed, rec, moment,
    local_sem, send_sem, recv_sem, init_send, init_recv, parcel_send, parcel_recv, relay_send, relay_recv,
    all_send, all_recv, token,
):
    s = lax.axis_index("shot")
    d = lax.axis_index("depth")
    shots, size = lax.axis_size("shot"), lax.axis_size("depth")
    rows_y, half = shots // Z_LO, size // 2
    y, z_lo, z_hi, x_core = s // Z_LO, lax.rem(s, Z_LO), d // half, lax.rem(d, half)
    chips_x, chips_z = half // 2, 2 * Z_LO
    x, z = x_core // 2, z_hi * Z_LO + z_lo
    odd = lax.rem(d, 2)
    early_side, late_side = 1 - odd, odd
    early_id = (s, d + 1 - 2 * odd)
    has_late = ((odd == 1) & (d < size - 1)) | ((odd == 0) & (d > 0))
    late_id = (s, jnp.clip(d - 1 + 2 * odd, 0, size - 1))

    def outward(count):
        return sorted(range(count), key=lambda r: -min(r, count - r))

    def y_peer(r):
        return (lax.rem(y + r, rows_y) * Z_LO + z_lo, d)

    far_side = (s, lax.rem(d + half, size))
    at_cut = (d == half - 1) | (d == half)

    barrier = pltpu.get_barrier_semaphore()

    def greet(device):
        pl.semaphore_signal(barrier, inc=1, device_id=device, device_id_type=MESH)

    @pl.when(at_cut)
    def _():
        greet((s, size - 1 - d))

    greet(far_side)
    for r in outward(rows_y)[:-1]:
        greet(y_peer(r))
    for r in range(1, Z_LO):
        greet((y * Z_LO + lax.rem(z_lo + r, Z_LO), d))
    for r in outward(half)[:-1]:
        greet((s, d - x_core + lax.rem(x_core + r, half)))

    data = pl.ds(PAD, ROWS)
    own = pl.ds(HALO, PLANES)
    loads = [
        pltpu.make_async_copy(fcur, u.at[1, :, own, data, :], local_sem.at[0]),
        pltpu.make_async_copy(fprev, u.at[0, :, own, data, :], local_sem.at[1]),
        pltpu.make_async_copy(c_in, cs.at[pl.ds(2, PLANES)], local_sem.at[2]),
        pltpu.make_async_copy(acur, stage_cur, local_sem.at[3]),
        pltpu.make_async_copy(anext, stage_next, local_sem.at[4]),
        pltpu.make_async_copy(observed_in, observed, local_sem.at[5]),
        pltpu.make_async_copy(rec_in, rec, local_sem.at[6]),
        pltpu.make_async_copy(moment_in, moment, local_sem.at[7]),
    ]
    for copy in loads:
        copy.start()

    pl.semaphore_wait(barrier, rows_y + Z_LO + half - 2 + jnp.where(at_cut, 1, 0))

    def copy_to(source, landing, send, recv, target):
        return pltpu.make_async_remote_copy(
            source, landing, send, recv, device_id=target, device_id_type=MESH
        )

    def first_copy(shot, side, target):
        return copy_to(
            fcur.at[shot, pl.ds((PLANES - 2) * side, 2)],
            u.at[1, shot, pl.ds(HALO - 2 + (PLANES + 2) * (1 - side), 2), data, :],
            init_send.at[shot, side], init_recv.at[shot, 1 - side], target,
        )

    def parcel(i, side):
        other = 1 - side
        if i == 0:
            return c_in.at[pl.ds((PLANES - 2) * side, 2)], cs.at[pl.ds((PLANES + 2) * other, 2)], relay.at[pl.ds(0, 2)]
        level, shot = (9, i - 1) if i < 3 else (8, i - 3)
        width = 2 if i < 3 else 4
        return (
            p.at[level, shot, pl.ds(HALO + (PLANES - width) * side, width), data, :],
            p.at[level, shot, pl.ds(HALO - width + (PLANES + width) * other, width), data, :],
            relay.at[pl.ds(2 * i if i < 3 else 4 * i - 6, width)],
        )

    def parcel_copy(i, side, target):
        source, landing, _ = parcel(i, side)
        return copy_to(source, landing, parcel_send.at[i, side], parcel_recv.at[i, 1 - side], target)

    relay_id = (s, jnp.where(d < half, 0, size - 1))
    relays = (d == 0) | (d == size - 1)

    def parcel_to_relay(i, side):
        source, _, middle = parcel(i, side)
        return copy_to(source, middle, parcel_send.at[i, side], relay_recv.at[i], relay_id)

    def parcel_from_relay(i, side):
        _, landing, middle = parcel(i, side)
        return copy_to(middle, landing, relay_send.at[i], parcel_recv.at[i, 1 - side], far_side)

    def post(items):
        for i in items:
            @pl.when(at_cut)
            def _():
                parcel_to_relay(i, late_side).start()

            @pl.when(has_late & jnp.logical_not(at_cut))
            def _():
                parcel_copy(i, late_side, late_id).start()

        for i in items:
            parcel_copy(i, early_side, early_id).start()

    def when_late(action):
        pl.when(has_late)(action)

    def halo_copy(buf, level, slot, shot, side, width, target):
        other = 1 - side
        return pltpu.make_async_remote_copy(
            buf.at[level, shot, pl.ds(HALO + (PLANES - width) * side, width), data, :],
            buf.at[level, shot, pl.ds(HALO - width + (PLANES + width) * other, width), data, :],
            send_sem.at[slot, shot, side],
            recv_sem.at[slot, shot, other],
            device_id=target,
            device_id_type=MESH,
        )

    for shot in range(SHOTS):
        when_late(lambda: first_copy(shot, late_side, late_id).start())
    for shot in range(SHOTS):
        first_copy(shot, early_side, early_id).start()
    post((0,))

    def pass_on(device):
        pl.semaphore_signal(token, inc=1, device_id=device, device_id_type=MESH)

    for r in outward(rows_y)[:-1]:
        pass_on(y_peer(r))
    pass_on(far_side)

    loads[2].wait()
    loads[3].wait()
    loads[4].wait()

    def scale(i, carry):
        factor = cs[2 + i]
        for shot in range(SHOTS):
            p[9, shot, HALO + i, PAD : PAD + ROWS, :] = factor * stage_next[shot, i]
            p[8, shot, HALO + i, PAD : PAD + ROWS, :] = factor * stage_cur[shot, i]
        return carry

    lax.fori_loop(0, PLANES, scale, 0)

    post(range(1, 5))

    def clear_pads(i, carry):
        level, plane = i // (PLANES + 2 * HALO), lax.rem(i, PLANES + 2 * HALO)
        zeros = jnp.zeros((PAD, LANES), jnp.float32)
        for buf in (u, p):
            for shot in range(SHOTS):
                buf[level, shot, plane, 0:PAD, :] = zeros
                buf[level, shot, plane, PAD + ROWS : 2 * PAD + ROWS, :] = zeros
        return carry

    lax.fori_loop(0, 10 * (PLANES + 2 * HALO), clear_pads, 0)

    @pl.when(jnp.logical_not(has_late))
    def _():
        first = (PLANES + HALO) * late_side

        def clear(i, carry):
            level, plane = i // HALO, first + lax.rem(i, HALO)
            zeros = jnp.zeros((ROWS, LANES), jnp.float32)
            for buf in (u, p):
                for shot in range(SHOTS):
                    buf[level, shot, plane, PAD : PAD + ROWS, :] = zeros
            return carry

        lax.fori_loop(0, 10 * HALO, clear, 0)
        for i in range(2):
            cs[(PLANES + 2) * late_side + i] = jnp.zeros((ROWS, LANES), jnp.float32)

    grad[...] = jnp.zeros_like(grad)

    for k in range(STEPS):
        cycle = lax.rem(ckpt[0] + k, 48).astype(jnp.float32)
        a = (jnp.full((1, LANES), cycle, jnp.float32) - 24.0) / 12.0
        wave[k : k + 1, :] = AMPLITUDE * (1.0 - 2.0 * a * a) * jnp.exp(-a * a)

    first_cell = (d * PLANES - 2) * (ROWS * LANES)
    rows_ext = EXT * ROWS
    row_at = lax.broadcasted_iota(jnp.int32, (rows_ext, NREC), 0)
    lane_at = lax.broadcasted_iota(jnp.int32, (LANES, NREC), 0)
    nt = (((1,), (1,)), ((), ()))

    def place(shot, carry):
        cell = rec[pl.ds(shot, 1), :] - first_cell
        row = lax.shift_right_arithmetic(cell, 7)
        lane = lax.bitwise_and(cell, 127)
        at_row = jnp.where(row_at == row, 1.0, 0.0).astype(jnp.bfloat16)
        lane_hit = lane_at == lane

        def put(values):
            right = jnp.where(lane_hit, values, 0.0).astype(jnp.bfloat16)
            return lax.dot_general(at_row, right, nt, preferred_element_type=jnp.float32)

        cnt[shot] = put(jnp.ones((1, NREC), jnp.float32)).reshape(EXT, ROWS, LANES)
        for k in range(STEPS):
            trace = observed[shot, k : k + 1, :]
            high = trace.astype(jnp.bfloat16).astype(jnp.float32)
            total = put(high) + put(trace - high)
            obs[k, shot] = total.reshape(EXT, ROWS, LANES)
        return carry

    cell_at = lax.broadcasted_iota(jnp.int32, (ROWS, LANES), 0) * LANES + lax.broadcasted_iota(jnp.int32, (ROWS, LANES), 1)
    for shot in range(SHOTS):
        source = src[shot] - first_cell
        for plane in range(EXT):
            hot[shot, plane] = jnp.where(cell_at == source - plane * (ROWS * LANES), 1.0, 0.0)

    lane_iota = lax.broadcasted_iota(jnp.int32, (ROWS, LANES), 1)
    masks = {j: (lane_iota >= j) if j > 0 else (lane_iota < LANES + j) for j in (1, 2, -1, -2)}

    def laplaces(buf, level, shot, start, count):
        def at(plane, dx):
            return buf[level, shot, start + plane, PAD + dx : PAD + dx + ROWS, :]

        def along_y(value, j):
            return jnp.where(masks[j], pltpu.roll(value, j % LANES, 1), 0.0)

        planes = {i: at(i, 0) for i in range(-2, count + 2)}
        out = []
        for i in range(count):
            center = planes[i]
            near = (planes[i - 1] + planes[i + 1]) + (at(i, -1) + at(i, 1)) + (along_y(center, 1) + along_y(center, -1))
            far = (planes[i - 2] + planes[i + 2]) + (at(i, -2) + at(i, 2)) + (along_y(center, 2) + along_y(center, -2))
            out.append((center, 3.0 * CENTER * center + NEAR * near + FAR * far))
        return out

    def forward(k, shot, start, count):
        strength = wave[pl.ds(k, 1), :]
        done = []
        for i, (center, value) in enumerate(laplaces(u, k + 1, shot, start, count)):
            plane = start + i
            value = value + strength * hot[shot, plane - 2]
            older = u[k, shot, plane, PAD : PAD + ROWS, :]
            done.append((plane, value, 2.0 * center - older + cs[plane - 2] * value))
        for plane, value, newer in done:
            lap[k, shot, plane - 2] = value
            u[k + 2, shot, plane, PAD : PAD + ROWS, :] = newer

    def backward(k, shot, start, count):
        done = []
        for i, (center, value) in enumerate(laplaces(p, k + 1, shot, start, count)):
            plane = start + i
            ahead = u[k + 2, shot, plane, PAD : PAD + ROWS, :]
            value = value + (cnt[shot, plane - 2] * ahead - obs[k, shot, plane - 2])
            later = p[k + 2, shot, plane, PAD : PAD + ROWS, :]
            newer = 2.0 * center - later + cs[plane - 2] * value
            done.append((plane, newer, grad[plane - 2] + newer * lap[k, shot, plane - 2]))
        for plane, newer, term in done:
            p[k, shot, plane, PAD : PAD + ROWS, :] = newer
            grad[plane - 2] = term

    even = 1 - odd
    loads[0].wait()
    loads[1].wait()

    def arrived(buf, level, slot, shot, side, width, target):
        halo_copy(buf, level, slot, shot, 1 - side, width, target).wait_recv()

    for shot in range(SHOTS):
        first_copy(shot, 1 - early_side, early_id).wait_recv()
        forward(0, shot, 4 + 2 * even, 6)
        halo_copy(u, 2, 0, shot, early_side, 4, early_id).start()
    for shot in range(SHOTS):
        when_late(lambda: first_copy(shot, 1 - late_side, late_id).wait_recv())
        forward(0, shot, 4 + 6 * odd, 2)
        when_late(lambda: halo_copy(u, 2, 0, shot, late_side, 4, late_id).start())

    for load in loads[5:]:
        load.wait()
    lax.fori_loop(0, SHOTS, place, 0)

    @pl.when(relays)
    def _():
        for i in range(5):
            parcel_to_relay(i, early_side).wait_recv()
            parcel_from_relay(i, early_side).start()

    parcel_copy(0, 1 - early_side, early_id).wait_recv()
    when_late(lambda: parcel_copy(0, 1 - late_side, late_id).wait_recv())

    def forward_round(j, carry):
        k = 2 * j + 1

        def leave(shot, side, target):
            @pl.when(j < 3)
            def _():
                halo_copy(u, k + 3, j + 1, shot, side, 4, target).start()

        def second(shot, start):
            @pl.when(j < 3)
            def _():
                forward(k + 1, shot, start, 4)

        for shot in range(SHOTS):
            arrived(u, k + 1, j, shot, early_side, 4, early_id)
            forward(k, shot, 2 + 4 * even, 8)
            second(shot, 4 + 4 * even)
            leave(shot, early_side, early_id)
        for shot in range(SHOTS):
            when_late(lambda: arrived(u, k + 1, j, shot, late_side, 4, late_id))
            forward(k, shot, 2 + 8 * odd, 4)
            second(shot, 4 + 4 * odd)
            when_late(lambda: leave(shot, late_side, late_id))
        return carry

    lax.fori_loop(0, 4, forward_round, 0)

    for i in range(1, 5):
        parcel_copy(i, 1 - early_side, early_id).wait_recv()
        when_late(lambda: parcel_copy(i, 1 - late_side, late_id).wait_recv())

    per_plane = shots // PLANES
    block_rows = ROWS // per_plane
    cells_all = size * PLANES * ROWS * LANES

    def remote(source, target, sem, device):
        return pltpu.make_async_remote_copy(
            source, target, all_send.at[sem], all_recv.at[sem], device_id=device, device_id_type=MESH
        )

    def scatter(side):
        first = (PLANES // 2) * side
        for i in range(PLANES // 2):
            blocks[pl.ds((first + i) * per_plane, per_plane)] = (grad[2 + first + i] / cs[2 + first + i]).reshape(
                per_plane, block_rows, LANES
            )

    pl.semaphore_wait(token, rows_y)

    def backward_round(i, carry):
        k = 7 - 2 * i

        def arrive(shot, side, target):
            @pl.when(i > 0)
            def _():
                arrived(p, k + 1, 3 + i, shot, side, 4, target)

        def leave(shot, side, target):
            @pl.when(i < 3)
            def _():
                halo_copy(p, k - 1, 4 + i, shot, side, 4, target).start()

        for shot in range(SHOTS):
            arrive(shot, early_side, early_id)
            backward(k, shot, 2 + 4 * even, 8)
            backward(k - 1, shot, 4 + 4 * even, 4)
            leave(shot, early_side, early_id)

        for shot in range(SHOTS):
            when_late(lambda: arrive(shot, late_side, late_id))
            backward(k, shot, 2 + 8 * odd, 4)
            backward(k - 1, shot, 4 + 4 * odd, 4)
            when_late(lambda: leave(shot, late_side, late_id))
        return carry

    lax.fori_loop(0, 4, backward_round, 0)

    scatter(late_side)
    scatter(early_side)

    def shot_peers():
        for dy in outward(rows_y):
            for dz in range(Z_LO):
                if dy or dz:
                    yield lax.rem(y + dy, rows_y) * Z_LO + lax.rem(z_lo + dz, Z_LO)

    others = pl.ds(0, shots - 1)
    for j in shot_peers():
        remote(blocks.at[j], parts.at[s], 0, (j, d)).start()
    parts[s] = blocks[s]
    remote(parts.at[others], parts.at[others], 0, (s, d)).wait_recv()
    total = lax.fori_loop(1, shots, lambda j, t: t + parts[j], parts[0])
    plane = d * PLANES + s // per_plane
    weight = 1.0 + 2.0 * plane.astype(jnp.float32) / (size * PLANES - 1)
    mine = weight * total
    scaled[s] = mine
    old = moment[s]
    squares = jnp.sum(mine * mine)

    column, plane_at = z * 2 + lax.rem(d, 2), y * chips_x + x
    for q, value in enumerate((squares, weight * jnp.sum(old * old), weight * jnp.sum(old * mine), weight * squares)):
        z_tiles[column, q : q + 1, :] = jnp.full((1, LANES), value, jnp.float32)
    z_tiles[column, 4:8, :] = jnp.zeros((4, LANES), jnp.float32)
    for dz in outward(chips_z):
        to_z = lax.rem(z + dz, chips_z)
        for flip in range(2):
            if dz or flip:
                core = lax.rem(d + flip, 2)
                device = (y * Z_LO + lax.rem(to_z, Z_LO), (to_z // Z_LO) * half + x * 2 + core)
                remote(z_tiles.at[column], z_tiles.at[column], 1, device).start()
    for j in shot_peers():
        remote(scaled.at[s], scaled.at[s], 2, (j, d)).start()
    others_z, others_xy = pl.ds(0, 2 * chips_z - 1), pl.ds(0, rows_y * chips_x - 1)
    remote(z_tiles.at[others_z], z_tiles.at[others_z], 1, (s, d)).wait_recv()
    xy_tiles[plane_at] = lax.fori_loop(1, 2 * chips_z, lambda j, t: t + z_tiles[j], z_tiles[0])
    for dy in outward(rows_y):
        for dx in outward(chips_x):
            if dy or dx:
                device = (lax.rem(y + dy, rows_y) * Z_LO + z_lo, z_hi * half + lax.rem(x + dx, chips_x) * 2 + lax.rem(d, 2))
                remote(xy_tiles.at[plane_at], xy_tiles.at[plane_at], 3, device).start()

    def sent(side, target):
        for i in range(5):
            parcel_copy(i, side, target).wait_send()
        for shot in range(SHOTS):
            first_copy(shot, side, target).wait_send()
            for slot, buf, level in ((0, u, 2), (1, u, 4), (2, u, 6), (3, u, 8), (4, p, 6), (5, p, 4), (6, p, 2)):
                halo_copy(buf, level, slot, shot, side, 4, target).wait_send()

    sent(early_side, early_id)
    when_late(lambda: sent(late_side, late_id))

    @pl.when(relays)
    def _():
        for i in range(5):
            parcel_from_relay(i, early_side).wait_send()

    remote(parts.at[others], parts.at[others], 0, (s, d)).wait_send()
    remote(z_tiles.at[others_z], z_tiles.at[others_z], 1, (s, d)).wait_send()
    remote(scaled.at[others], scaled.at[others], 2, (s, d)).wait_send()
    remote(xy_tiles.at[others_xy], xy_tiles.at[others_xy], 3, (s, d)).wait_send()
    remote(xy_tiles.at[others_xy], xy_tiles.at[others_xy], 3, (s, d)).wait_recv()
    grand = lax.fori_loop(1, rows_y * chips_x, lambda j, t: t + xy_tiles[j], xy_tiles[0])
    step = 0.5 * lax.rsqrt(grand[0:1, :] / cells_all + EPSILON)
    energy = grand[1:2, :] - 2.0 * step * grand[2:3, :] + step * step * grand[3:4, :]
    kinetic_out[...] = 0.5 * energy / cells_all
    remote(scaled.at[others], scaled.at[others], 2, (s, d)).wait_recv()

    def update(j, carry):
        half_out[j] = moment[j] - step * scaled[j]
        return carry

    lax.fori_loop(0, shots, update, 0)


def window(c, momentum, fprev, fcur, anext, acur, observed, src, rec, ckpt, ns, nd):
    any_space = pl.BlockSpec(memory_space=pl.ANY)
    in_vmem = pl.BlockSpec(memory_space=pltpu.VMEM)
    in_smem = pl.BlockSpec(memory_space=pltpu.SMEM)
    padded = (10, SHOTS, PLANES + 2 * HALO, ROWS + 2 * PAD, LANES)
    f32 = jnp.float32
    blocks = (ns, PLANES * ROWS // ns, LANES)
    half, kinetic = pl.pallas_call(
        window_kernel,
        out_shape=(jax.ShapeDtypeStruct(blocks, f32), jax.ShapeDtypeStruct((1, LANES), f32)),
        in_specs=[any_space] * 6 + [in_smem, any_space, in_smem, any_space],
        out_specs=(in_vmem, in_vmem),
        scratch_shapes=[
            pltpu.VMEM(padded, f32),
            pltpu.VMEM(padded, f32),
            pltpu.VMEM((STEPS, SHOTS, EXT, ROWS, LANES), f32),
            pltpu.VMEM((STEPS, SHOTS, EXT, ROWS, LANES), f32),
            pltpu.VMEM((SHOTS, EXT, ROWS, LANES), f32),
            pltpu.VMEM((SHOTS, EXT, ROWS, LANES), f32),
            pltpu.VMEM((EXT, ROWS, LANES), f32),
            pltpu.VMEM((EXT, ROWS, LANES), f32),
            pltpu.VMEM((STEPS, LANES), f32),
            pltpu.VMEM((SHOTS, PLANES, ROWS, LANES), f32),
            pltpu.VMEM((SHOTS, PLANES, ROWS, LANES), f32),
            pltpu.VMEM(blocks, f32),
            pltpu.VMEM(blocks, f32),
            pltpu.VMEM(blocks, f32),
            pltpu.VMEM((4 * Z_LO, 8, LANES), f32),
            pltpu.VMEM((ns // Z_LO * nd // 4, 8, LANES), f32),
            pltpu.VMEM((14, ROWS, LANES), f32),
            pltpu.VMEM((SHOTS, STEPS, NREC), f32),
            pltpu.VMEM((SHOTS, NREC), jnp.int32),
            pltpu.VMEM(blocks, f32),
            pltpu.SemaphoreType.DMA((8,)),
            pltpu.SemaphoreType.DMA((7, SHOTS, 2)),
            pltpu.SemaphoreType.DMA((7, SHOTS, 2)),
            pltpu.SemaphoreType.DMA((SHOTS, 2)),
            pltpu.SemaphoreType.DMA((SHOTS, 2)),
            pltpu.SemaphoreType.DMA((5, 2)),
            pltpu.SemaphoreType.DMA((5, 2)),
            pltpu.SemaphoreType.DMA((5,)),
            pltpu.SemaphoreType.DMA((5,)),
            pltpu.SemaphoreType.DMA((4,)),
            pltpu.SemaphoreType.DMA((4,)),
            pltpu.SemaphoreType.REGULAR,
        ],
        compiler_params=pltpu.CompilerParams(
            collective_id=0, has_side_effects=True, vmem_limit_bytes=60 * 1024 * 1024
        ),
        name="window",
    )(c, fprev, fcur, anext, acur, observed, src, rec, ckpt, momentum.reshape(blocks))
    return half.reshape(momentum.shape), kinetic[0, 0]


def solution(mesh):
    def shards(c, momentum, fprev, fcur, anext, acur, observed, src, rec, ckpt):
        return window(
            c, momentum, fprev, fcur, anext, acur, observed, src, rec, ckpt.reshape(1),
            mesh.shape["shot"], mesh.shape["depth"],
        )

    placed = (
        P("depth", None, None),
        P("depth", None, None),
        P("shot", "depth", None, None),
        P("shot", "depth", None, None),
        P("shot", "depth", None, None),
        P("shot", "depth", None, None),
        P("shot", None, None),
        P("shot"),
        P("shot", None),
        P(),
    )
    return jax.shard_map(
        shards, mesh=mesh, in_specs=placed, out_specs=(P("depth", None, None), P()), check_vma=False
    )
```

```python
import jax
import jax.numpy as jnp
from jax import lax
from jax.experimental import pallas as pl
from jax.experimental.pallas import tpu as pltpu
from jax.sharding import PartitionSpec as P

MESH = pl.DeviceIdType.MESH
CENTER = -2.5
NEAR = 4.0 / 3.0
FAR = -1.0 / 12.0
AMPLITUDE = 100.0
EPSILON = 1e-06

SHOTS = 2
PLANES = 8
ROWS = 64
LANES = 128
STEPS = 8
HALO = 4
PAD = 8
EXT = PLANES + 4
NREC = 512
Z_LO = 4


def window_kernel(
    c_in, fprev, fcur, anext, acur, observed_in, src, rec_in, ckpt, moment_in,
    half_out, kinetic_out,
    u, p, lap, obs, cnt, hot, cs, grad, wave, stage_next, stage_cur,
    blocks, parts, scaled, z_tiles, xy_tiles,
    relay, observed, rec, moment, lines, line_parts,
    local_sem, send_sem, recv_sem, init_send, init_recv, parcel_send, parcel_recv, relay_send, relay_recv,
    all_send, all_recv, token,
):
    s = lax.axis_index("shot")
    d = lax.axis_index("depth")
    shots, size = lax.axis_size("shot"), lax.axis_size("depth")
    rows_y, half = shots // Z_LO, size // 2
    y, z_lo, z_hi, x_core = s // Z_LO, lax.rem(s, Z_LO), d // half, lax.rem(d, half)
    chips_x, chips_z = half // 2, 2 * Z_LO
    x, z = x_core // 2, z_hi * Z_LO + z_lo
    odd = lax.rem(d, 2)
    early_side, late_side = 1 - odd, odd
    early_id = (s, d + 1 - 2 * odd)
    has_late = ((odd == 1) & (d < size - 1)) | ((odd == 0) & (d > 0))
    late_id = (s, jnp.clip(d - 1 + 2 * odd, 0, size - 1))

    def outward(count):
        return sorted(range(count), key=lambda r: -min(r, count - r))

    def y_peer(r):
        return (lax.rem(y + r, rows_y) * Z_LO + z_lo, d)

    far_side = (s, lax.rem(d + half, size))
    at_cut = (d == half - 1) | (d == half)

    barrier = pltpu.get_barrier_semaphore()

    def greet(device):
        pl.semaphore_signal(barrier, inc=1, device_id=device, device_id_type=MESH)

    @pl.when(at_cut)
    def _():
        greet((s, size - 1 - d))

    greet(far_side)
    for r in outward(rows_y)[:-1]:
        greet(y_peer(r))
    for r in range(1, Z_LO):
        greet((y * Z_LO + lax.rem(z_lo + r, Z_LO), d))
    for r in outward(half)[:-1]:
        greet((s, d - x_core + lax.rem(x_core + r, half)))

    data = pl.ds(PAD, ROWS)
    own = pl.ds(HALO, PLANES)
    loads = [
        pltpu.make_async_copy(fcur, u.at[1, :, own, data, :], local_sem.at[0]),
        pltpu.make_async_copy(fprev, u.at[0, :, own, data, :], local_sem.at[1]),
        pltpu.make_async_copy(c_in, cs.at[pl.ds(2, PLANES)], local_sem.at[2]),
        pltpu.make_async_copy(acur, stage_cur, local_sem.at[3]),
        pltpu.make_async_copy(anext, stage_next, local_sem.at[4]),
        pltpu.make_async_copy(observed_in, observed, local_sem.at[5]),
        pltpu.make_async_copy(rec_in, rec, local_sem.at[6]),
        pltpu.make_async_copy(moment_in, moment, local_sem.at[7]),
    ]
    for copy in loads:
        copy.start()

    pl.semaphore_wait(barrier, rows_y + Z_LO + half - 2 + jnp.where(at_cut, 1, 0))

    def copy_to(source, landing, send, recv, target):
        return pltpu.make_async_remote_copy(
            source, landing, send, recv, device_id=target, device_id_type=MESH
        )

    def first_copy(shot, side, target):
        return copy_to(
            fcur.at[shot, pl.ds((PLANES - 2) * side, 2)],
            u.at[1, shot, pl.ds(HALO - 2 + (PLANES + 2) * (1 - side), 2), data, :],
            init_send.at[shot, side], init_recv.at[shot, 1 - side], target,
        )

    def parcel(i, side):
        other = 1 - side
        if i == 0:
            return c_in.at[pl.ds((PLANES - 2) * side, 2)], cs.at[pl.ds((PLANES + 2) * other, 2)], relay.at[pl.ds(0, 2)]
        level, shot = (9, i - 1) if i < 3 else (8, i - 3)
        width = 2 if i < 3 else 4
        return (
            p.at[level, shot, pl.ds(HALO + (PLANES - width) * side, width), data, :],
            p.at[level, shot, pl.ds(HALO - width + (PLANES + width) * other, width), data, :],
            relay.at[pl.ds(2 * i if i < 3 else 4 * i - 6, width)],
        )

    def parcel_copy(i, side, target):
        source, landing, _ = parcel(i, side)
        return copy_to(source, landing, parcel_send.at[i, side], parcel_recv.at[i, 1 - side], target)

    relay_id = (s, jnp.where(d < half, 0, size - 1))
    relays = (d == 0) | (d == size - 1)

    def parcel_to_relay(i, side):
        source, _, middle = parcel(i, side)
        return copy_to(source, middle, parcel_send.at[i, side], relay_recv.at[i], relay_id)

    def parcel_from_relay(i, side):
        _, landing, middle = parcel(i, side)
        return copy_to(middle, landing, relay_send.at[i], parcel_recv.at[i, 1 - side], far_side)

    def post(items):
        for i in items:
            @pl.when(at_cut)
            def _():
                parcel_to_relay(i, late_side).start()

            @pl.when(has_late & jnp.logical_not(at_cut))
            def _():
                parcel_copy(i, late_side, late_id).start()

        for i in items:
            parcel_copy(i, early_side, early_id).start()

    def when_late(action):
        pl.when(has_late)(action)

    def halo_copy(buf, level, slot, shot, side, width, target):
        other = 1 - side
        return pltpu.make_async_remote_copy(
            buf.at[level, shot, pl.ds(HALO + (PLANES - width) * side, width), data, :],
            buf.at[level, shot, pl.ds(HALO - width + (PLANES + width) * other, width), data, :],
            send_sem.at[slot, shot, side],
            recv_sem.at[slot, shot, other],
            device_id=target,
            device_id_type=MESH,
        )

    for shot in range(SHOTS):
        when_late(lambda: first_copy(shot, late_side, late_id).start())
    for shot in range(SHOTS):
        first_copy(shot, early_side, early_id).start()
    post((0,))

    def pass_on(device):
        pl.semaphore_signal(token, inc=1, device_id=device, device_id_type=MESH)

    for r in outward(rows_y)[:-1]:
        pass_on(y_peer(r))
    pass_on(far_side)

    loads[2].wait()
    loads[3].wait()
    loads[4].wait()

    def scale(i, carry):
        factor = cs[2 + i]
        for shot in range(SHOTS):
            p[9, shot, HALO + i, PAD : PAD + ROWS, :] = factor * stage_next[shot, i]
            p[8, shot, HALO + i, PAD : PAD + ROWS, :] = factor * stage_cur[shot, i]
        return carry

    lax.fori_loop(0, PLANES, scale, 0)

    post(range(1, 5))

    def clear_pads(i, carry):
        level, plane = i // (PLANES + 2 * HALO), lax.rem(i, PLANES + 2 * HALO)
        zeros = jnp.zeros((PAD, LANES), jnp.float32)
        for buf in (u, p):
            for shot in range(SHOTS):
                buf[level, shot, plane, 0:PAD, :] = zeros
                buf[level, shot, plane, PAD + ROWS : 2 * PAD + ROWS, :] = zeros
        return carry

    lax.fori_loop(0, 10 * (PLANES + 2 * HALO), clear_pads, 0)

    @pl.when(jnp.logical_not(has_late))
    def _():
        first = (PLANES + HALO) * late_side

        def clear(i, carry):
            level, plane = i // HALO, first + lax.rem(i, HALO)
            zeros = jnp.zeros((ROWS, LANES), jnp.float32)
            for buf in (u, p):
                for shot in range(SHOTS):
                    buf[level, shot, plane, PAD : PAD + ROWS, :] = zeros
            return carry

        lax.fori_loop(0, 10 * HALO, clear, 0)
        for i in range(2):
            cs[(PLANES + 2) * late_side + i] = jnp.zeros((ROWS, LANES), jnp.float32)

    grad[...] = jnp.zeros_like(grad)

    for k in range(STEPS):
        cycle = lax.rem(ckpt[0] + k, 48).astype(jnp.float32)
        a = (jnp.full((1, LANES), cycle, jnp.float32) - 24.0) / 12.0
        wave[k : k + 1, :] = AMPLITUDE * (1.0 - 2.0 * a * a) * jnp.exp(-a * a)

    first_cell = (d * PLANES - 2) * (ROWS * LANES)
    rows_ext = EXT * ROWS
    row_at = lax.broadcasted_iota(jnp.int32, (rows_ext, NREC), 0)
    lane_at = lax.broadcasted_iota(jnp.int32, (LANES, NREC), 0)
    nt = (((1,), (1,)), ((), ()))

    def place(shot, carry):
        cell = rec[pl.ds(shot, 1), :] - first_cell
        row = lax.shift_right_arithmetic(cell, 7)
        lane = lax.bitwise_and(cell, 127)
        at_row = jnp.where(row_at == row, 1.0, 0.0).astype(jnp.bfloat16)
        lane_hit = lane_at == lane

        def put(values):
            right = jnp.where(lane_hit, values, 0.0).astype(jnp.bfloat16)
            return lax.dot_general(at_row, right, nt, preferred_element_type=jnp.float32)

        cnt[shot] = put(jnp.ones((1, NREC), jnp.float32)).reshape(EXT, ROWS, LANES)
        for k in range(STEPS):
            trace = observed[shot, k : k + 1, :]
            high = trace.astype(jnp.bfloat16).astype(jnp.float32)
            total = put(high) + put(trace - high)
            obs[k, shot] = total.reshape(EXT, ROWS, LANES)
        return carry

    cell_at = lax.broadcasted_iota(jnp.int32, (ROWS, LANES), 0) * LANES + lax.broadcasted_iota(jnp.int32, (ROWS, LANES), 1)
    for shot in range(SHOTS):
        source = src[shot] - first_cell
        for plane in range(EXT):
            hot[shot, plane] = jnp.where(cell_at == source - plane * (ROWS * LANES), 1.0, 0.0)

    lane_iota = lax.broadcasted_iota(jnp.int32, (ROWS, LANES), 1)
    masks = {j: (lane_iota >= j) if j > 0 else (lane_iota < LANES + j) for j in (1, 2, -1, -2)}

    def laplaces(buf, level, shot, start, count):
        def at(plane, dx):
            return buf[level, shot, start + plane, PAD + dx : PAD + dx + ROWS, :]

        def along_y(value, j):
            return jnp.where(masks[j], pltpu.roll(value, j % LANES, 1), 0.0)

        planes = {i: at(i, 0) for i in range(-2, count + 2)}
        out = []
        for i in range(count):
            center = planes[i]
            near = (planes[i - 1] + planes[i + 1]) + (at(i, -1) + at(i, 1)) + (along_y(center, 1) + along_y(center, -1))
            far = (planes[i - 2] + planes[i + 2]) + (at(i, -2) + at(i, 2)) + (along_y(center, 2) + along_y(center, -2))
            out.append((center, 3.0 * CENTER * center + NEAR * near + FAR * far))
        return out

    def forward(k, shot, start, count):
        strength = wave[pl.ds(k, 1), :]
        done = []
        for i, (center, value) in enumerate(laplaces(u, k + 1, shot, start, count)):
            plane = start + i
            value = value + strength * hot[shot, plane - 2]
            older = u[k, shot, plane, PAD : PAD + ROWS, :]
            done.append((plane, value, 2.0 * center - older + cs[plane - 2] * value))
        for plane, value, newer in done:
            lap[k, shot, plane - 2] = value
            u[k + 2, shot, plane, PAD : PAD + ROWS, :] = newer

    def backward(k, shot, start, count):
        done = []
        for i, (center, value) in enumerate(laplaces(p, k + 1, shot, start, count)):
            plane = start + i
            ahead = u[k + 2, shot, plane, PAD : PAD + ROWS, :]
            value = value + (cnt[shot, plane - 2] * ahead - obs[k, shot, plane - 2])
            later = p[k + 2, shot, plane, PAD : PAD + ROWS, :]
            newer = 2.0 * center - later + cs[plane - 2] * value
            done.append((plane, newer, grad[plane - 2] + newer * lap[k, shot, plane - 2]))
        for plane, newer, term in done:
            p[k, shot, plane, PAD : PAD + ROWS, :] = newer
            grad[plane - 2] = term

    even = 1 - odd
    loads[0].wait()
    loads[1].wait()

    def arrived(buf, level, slot, shot, side, width, target):
        halo_copy(buf, level, slot, shot, 1 - side, width, target).wait_recv()

    for shot in range(SHOTS):
        first_copy(shot, 1 - early_side, early_id).wait_recv()
        forward(0, shot, 4 + 2 * even, 6)
        halo_copy(u, 2, 0, shot, early_side, 4, early_id).start()
    for shot in range(SHOTS):
        when_late(lambda: first_copy(shot, 1 - late_side, late_id).wait_recv())
        forward(0, shot, 4 + 6 * odd, 2)
        when_late(lambda: halo_copy(u, 2, 0, shot, late_side, 4, late_id).start())

    for load in loads[5:]:
        load.wait()
    lax.fori_loop(0, SHOTS, place, 0)

    @pl.when(relays)
    def _():
        for i in range(5):
            parcel_to_relay(i, early_side).wait_recv()
            parcel_from_relay(i, early_side).start()

    parcel_copy(0, 1 - early_side, early_id).wait_recv()
    when_late(lambda: parcel_copy(0, 1 - late_side, late_id).wait_recv())

    def forward_round(j, carry):
        k = 2 * j + 1

        def leave(shot, side, target):
            @pl.when(j < 3)
            def _():
                halo_copy(u, k + 3, j + 1, shot, side, 4, target).start()

        def second(shot, start):
            @pl.when(j < 3)
            def _():
                forward(k + 1, shot, start, 4)

        for shot in range(SHOTS):
            arrived(u, k + 1, j, shot, early_side, 4, early_id)
            forward(k, shot, 2 + 4 * even, 8)
            second(shot, 4 + 4 * even)
            leave(shot, early_side, early_id)
        for shot in range(SHOTS):
            when_late(lambda: arrived(u, k + 1, j, shot, late_side, 4, late_id))
            forward(k, shot, 2 + 8 * odd, 4)
            second(shot, 4 + 4 * odd)
            when_late(lambda: leave(shot, late_side, late_id))
        return carry

    lax.fori_loop(0, 4, forward_round, 0)

    for i in range(1, 5):
        parcel_copy(i, 1 - early_side, early_id).wait_recv()
        when_late(lambda: parcel_copy(i, 1 - late_side, late_id).wait_recv())

    per_plane = shots // PLANES
    block_rows = ROWS // per_plane
    cells_all = size * PLANES * ROWS * LANES

    def remote(source, target, sem, device):
        return pltpu.make_async_remote_copy(
            source, target, all_send.at[sem], all_recv.at[sem], device_id=device, device_id_type=MESH
        )

    def scatter(side):
        first = (PLANES // 2) * side
        for i in range(PLANES // 2):
            blocks[pl.ds((first + i) * per_plane, per_plane)] = (grad[2 + first + i] / cs[2 + first + i]).reshape(
                per_plane, block_rows, LANES
            )

    pl.semaphore_wait(token, rows_y)

    def backward_round(i, carry):
        k = 7 - 2 * i

        def arrive(shot, side, target):
            @pl.when(i > 0)
            def _():
                arrived(p, k + 1, 3 + i, shot, side, 4, target)

        def leave(shot, side, target):
            @pl.when(i < 3)
            def _():
                halo_copy(p, k - 1, 4 + i, shot, side, 4, target).start()

        for shot in range(SHOTS):
            arrive(shot, early_side, early_id)
            backward(k, shot, 2 + 4 * even, 8)
            backward(k - 1, shot, 4 + 4 * even, 4)
            leave(shot, early_side, early_id)

        for shot in range(SHOTS):
            when_late(lambda: arrive(shot, late_side, late_id))
            backward(k, shot, 2 + 8 * odd, 4)
            backward(k - 1, shot, 4 + 4 * odd, 4)
            when_late(lambda: leave(shot, late_side, late_id))
        return carry

    lax.fori_loop(0, 4, backward_round, 0)

    scatter(late_side)
    scatter(early_side)

    def shot_peers():
        for dy in outward(rows_y):
            for dz in range(Z_LO):
                if dy or dz:
                    yield lax.rem(y + dy, rows_y) * Z_LO + lax.rem(z_lo + dz, Z_LO)

    others = pl.ds(0, shots - 1)
    plane = d * PLANES + s // per_plane
    weight = 1.0 + 2.0 * plane.astype(jnp.float32) / (size * PLANES - 1)
    off_cut = jnp.logical_not(at_cut)
    line = pl.ds(y * Z_LO, Z_LO)
    others_y, others_line = pl.ds(0, (rows_y - 1) * Z_LO), pl.ds(0, Z_LO - 1)

    def z_peers():
        for r in range(1, Z_LO):
            to = lax.rem(z_lo + r, Z_LO)
            yield to, (y * Z_LO + to, d)

    @pl.when(at_cut)
    def _():
        for j in shot_peers():
            remote(blocks.at[j], parts.at[s], 0, (j, d)).start()
        parts[s] = blocks[s]
        remote(parts.at[others], parts.at[others], 0, (s, d)).wait_recv()
        scaled[s] = weight * lax.fori_loop(1, shots, lambda j, t: t + parts[j], parts[0])

    @pl.when(off_cut)
    def _():
        for r in outward(rows_y)[:-1]:
            to = lax.rem(y + r, rows_y)
            remote(blocks.at[pl.ds(to * Z_LO, Z_LO)], parts.at[line], 4, y_peer(r)).start()
        parts[line] = blocks[line]
        remote(parts.at[others_y], parts.at[others_y], 4, (s, d)).wait_recv()
        lines[...] = lax.fori_loop(1, rows_y, lambda j, t: t + parts[pl.ds(j * Z_LO, Z_LO)], parts[0:Z_LO])
        for to, device in z_peers():
            remote(lines.at[to], line_parts.at[z_lo], 5, device).start()
        line_parts[z_lo] = lines[z_lo]
        remote(line_parts.at[others_line], line_parts.at[others_line], 5, (s, d)).wait_recv()
        scaled[s] = weight * lax.fori_loop(1, Z_LO, lambda j, t: t + line_parts[j], line_parts[0])

    mine = scaled[s]
    old = moment[s]
    squares = jnp.sum(mine * mine)

    column, plane_at = z * 2 + lax.rem(d, 2), y * chips_x + x
    for q, value in enumerate((squares, weight * jnp.sum(old * old), weight * jnp.sum(old * mine), weight * squares)):
        z_tiles[column, q : q + 1, :] = jnp.full((1, LANES), value, jnp.float32)
    z_tiles[column, 4:8, :] = jnp.zeros((4, LANES), jnp.float32)
    for dz in outward(chips_z):
        to_z = lax.rem(z + dz, chips_z)
        for flip in range(2):
            if dz or flip:
                core = lax.rem(d + flip, 2)
                device = (y * Z_LO + lax.rem(to_z, Z_LO), (to_z // Z_LO) * half + x * 2 + core)
                remote(z_tiles.at[column], z_tiles.at[column], 1, device).start()

    @pl.when(at_cut)
    def _():
        for j in shot_peers():
            remote(scaled.at[s], scaled.at[s], 2, (j, d)).start()

    @pl.when(off_cut)
    def _():
        for _, device in z_peers():
            remote(scaled.at[s], scaled.at[s], 6, device).start()
        remote(scaled.at[others_line], scaled.at[others_line], 6, (s, d)).wait_recv()
        for r in outward(rows_y)[:-1]:
            remote(scaled.at[line], scaled.at[line], 2, y_peer(r)).start()

    others_z, others_xy = pl.ds(0, 2 * chips_z - 1), pl.ds(0, rows_y * chips_x - 1)
    remote(z_tiles.at[others_z], z_tiles.at[others_z], 1, (s, d)).wait_recv()
    xy_tiles[plane_at] = lax.fori_loop(1, 2 * chips_z, lambda j, t: t + z_tiles[j], z_tiles[0])
    for dy in outward(rows_y):
        for dx in outward(chips_x):
            if dy or dx:
                device = (lax.rem(y + dy, rows_y) * Z_LO + z_lo, z_hi * half + lax.rem(x + dx, chips_x) * 2 + lax.rem(d, 2))
                remote(xy_tiles.at[plane_at], xy_tiles.at[plane_at], 3, device).start()

    def sent(side, target):
        for i in range(5):
            parcel_copy(i, side, target).wait_send()
        for shot in range(SHOTS):
            first_copy(shot, side, target).wait_send()
            for slot, buf, level in ((0, u, 2), (1, u, 4), (2, u, 6), (3, u, 8), (4, p, 6), (5, p, 4), (6, p, 2)):
                halo_copy(buf, level, slot, shot, side, 4, target).wait_send()

    sent(early_side, early_id)
    when_late(lambda: sent(late_side, late_id))

    @pl.when(relays)
    def _():
        for i in range(5):
            parcel_from_relay(i, early_side).wait_send()

    @pl.when(at_cut)
    def _():
        remote(parts.at[others], parts.at[others], 0, (s, d)).wait_send()
        remote(scaled.at[others], scaled.at[others], 2, (s, d)).wait_send()

    @pl.when(off_cut)
    def _():
        remote(parts.at[others_y], parts.at[others_y], 4, (s, d)).wait_send()
        remote(line_parts.at[others_line], line_parts.at[others_line], 5, (s, d)).wait_send()
        remote(scaled.at[others_line], scaled.at[others_line], 6, (s, d)).wait_send()
        remote(scaled.at[others_y], scaled.at[others_y], 2, (s, d)).wait_send()

    remote(z_tiles.at[others_z], z_tiles.at[others_z], 1, (s, d)).wait_send()
    remote(xy_tiles.at[others_xy], xy_tiles.at[others_xy], 3, (s, d)).wait_send()
    remote(xy_tiles.at[others_xy], xy_tiles.at[others_xy], 3, (s, d)).wait_recv()
    grand = lax.fori_loop(1, rows_y * chips_x, lambda j, t: t + xy_tiles[j], xy_tiles[0])
    step = 0.5 * lax.rsqrt(grand[0:1, :] / cells_all + EPSILON)
    energy = grand[1:2, :] - 2.0 * step * grand[2:3, :] + step * step * grand[3:4, :]
    kinetic_out[...] = 0.5 * energy / cells_all

    @pl.when(at_cut)
    def _():
        remote(scaled.at[others], scaled.at[others], 2, (s, d)).wait_recv()

    @pl.when(off_cut)
    def _():
        remote(scaled.at[others_y], scaled.at[others_y], 2, (s, d)).wait_recv()

    def update(j, carry):
        half_out[j] = moment[j] - step * scaled[j]
        return carry

    lax.fori_loop(0, shots, update, 0)


def window(c, momentum, fprev, fcur, anext, acur, observed, src, rec, ckpt, ns, nd):
    any_space = pl.BlockSpec(memory_space=pl.ANY)
    in_vmem = pl.BlockSpec(memory_space=pltpu.VMEM)
    in_smem = pl.BlockSpec(memory_space=pltpu.SMEM)
    padded = (10, SHOTS, PLANES + 2 * HALO, ROWS + 2 * PAD, LANES)
    f32 = jnp.float32
    blocks = (ns, PLANES * ROWS // ns, LANES)
    half, kinetic = pl.pallas_call(
        window_kernel,
        out_shape=(jax.ShapeDtypeStruct(blocks, f32), jax.ShapeDtypeStruct((1, LANES), f32)),
        in_specs=[any_space] * 6 + [in_smem, any_space, in_smem, any_space],
        out_specs=(in_vmem, in_vmem),
        scratch_shapes=[
            pltpu.VMEM(padded, f32),
            pltpu.VMEM(padded, f32),
            pltpu.VMEM((STEPS, SHOTS, EXT, ROWS, LANES), f32),
            pltpu.VMEM((STEPS, SHOTS, EXT, ROWS, LANES), f32),
            pltpu.VMEM((SHOTS, EXT, ROWS, LANES), f32),
            pltpu.VMEM((SHOTS, EXT, ROWS, LANES), f32),
            pltpu.VMEM((EXT, ROWS, LANES), f32),
            pltpu.VMEM((EXT, ROWS, LANES), f32),
            pltpu.VMEM((STEPS, LANES), f32),
            pltpu.VMEM((SHOTS, PLANES, ROWS, LANES), f32),
            pltpu.VMEM((SHOTS, PLANES, ROWS, LANES), f32),
            pltpu.VMEM(blocks, f32),
            pltpu.VMEM(blocks, f32),
            pltpu.VMEM(blocks, f32),
            pltpu.VMEM((4 * Z_LO, 8, LANES), f32),
            pltpu.VMEM((ns // Z_LO * nd // 4, 8, LANES), f32),
            pltpu.VMEM((14, ROWS, LANES), f32),
            pltpu.VMEM((SHOTS, STEPS, NREC), f32),
            pltpu.VMEM((SHOTS, NREC), jnp.int32),
            pltpu.VMEM(blocks, f32),
            pltpu.VMEM((Z_LO,) + blocks[1:], f32),
            pltpu.VMEM((Z_LO,) + blocks[1:], f32),
            pltpu.SemaphoreType.DMA((8,)),
            pltpu.SemaphoreType.DMA((7, SHOTS, 2)),
            pltpu.SemaphoreType.DMA((7, SHOTS, 2)),
            pltpu.SemaphoreType.DMA((SHOTS, 2)),
            pltpu.SemaphoreType.DMA((SHOTS, 2)),
            pltpu.SemaphoreType.DMA((5, 2)),
            pltpu.SemaphoreType.DMA((5, 2)),
            pltpu.SemaphoreType.DMA((5,)),
            pltpu.SemaphoreType.DMA((5,)),
            pltpu.SemaphoreType.DMA((7,)),
            pltpu.SemaphoreType.DMA((7,)),
            pltpu.SemaphoreType.REGULAR,
        ],
        compiler_params=pltpu.CompilerParams(
            collective_id=0, has_side_effects=True, vmem_limit_bytes=60 * 1024 * 1024
        ),
        name="window",
    )(c, fprev, fcur, anext, acur, observed, src, rec, ckpt, momentum.reshape(blocks))
    return half.reshape(momentum.shape), kinetic[0, 0]


def solution(mesh):
    def shards(c, momentum, fprev, fcur, anext, acur, observed, src, rec, ckpt):
        return window(
            c, momentum, fprev, fcur, anext, acur, observed, src, rec, ckpt.reshape(1),
            mesh.shape["shot"], mesh.shape["depth"],
        )

    placed = (
        P("depth", None, None),
        P("depth", None, None),
        P("shot", "depth", None, None),
        P("shot", "depth", None, None),
        P("shot", "depth", None, None),
        P("shot", "depth", None, None),
        P("shot", None, None),
        P("shot"),
        P("shot", None),
        P(),
    )
    return jax.shard_map(
        shards, mesh=mesh, in_specs=placed, out_specs=(P("depth", None, None), P()), check_vma=False
    )
```

```python
import jax
import jax.numpy as jnp
from jax import lax
from jax.experimental import pallas as pl
from jax.experimental.pallas import tpu as pltpu
from jax.sharding import PartitionSpec as P

MESH = pl.DeviceIdType.MESH
CENTER = -2.5
NEAR = 4.0 / 3.0
FAR = -1.0 / 12.0
AMPLITUDE = 100.0
EPSILON = 1e-06

SHOTS = 2
PLANES = 8
ROWS = 64
LANES = 128
STEPS = 8
HALO = 4
PAD = 8
EXT = PLANES + 4
NREC = 512
Z_LO = 4


def window_kernel(
    c_in, fprev, fcur, anext, acur, observed_in, src, rec_in, ckpt, moment_in,
    half_out, kinetic_out,
    u, p, lap, obs, cnt, hot, cs, grad, wave, stage_next, stage_cur,
    blocks, parts, scaled, z_tiles, xy_tiles,
    relay, observed, rec, moment, lines, line_parts,
    local_sem, send_sem, recv_sem, init_send, init_recv, parcel_send, parcel_recv, relay_send, relay_recv,
    all_send, all_recv, token,
):
    s = lax.axis_index("shot")
    d = lax.axis_index("depth")
    shots, size = lax.axis_size("shot"), lax.axis_size("depth")
    rows_y, half = shots // Z_LO, size // 2
    y, z_lo, z_hi, x_core = s // Z_LO, lax.rem(s, Z_LO), d // half, lax.rem(d, half)
    chips_x, chips_z = half // 2, 2 * Z_LO
    x, z = x_core // 2, z_hi * Z_LO + z_lo
    odd = lax.rem(d, 2)
    early_side, late_side = 1 - odd, odd
    early_id = (s, d + 1 - 2 * odd)
    has_late = ((odd == 1) & (d < size - 1)) | ((odd == 0) & (d > 0))
    late_id = (s, jnp.clip(d - 1 + 2 * odd, 0, size - 1))

    def outward(count):
        return sorted(range(count), key=lambda r: -min(r, count - r))

    def y_peer(r):
        return (lax.rem(y + r, rows_y) * Z_LO + z_lo, d)

    far_side = (s, lax.rem(d + half, size))
    at_cut = (d == half - 1) | (d == half)

    barrier = pltpu.get_barrier_semaphore()

    def greet(device):
        pl.semaphore_signal(barrier, inc=1, device_id=device, device_id_type=MESH)

    @pl.when(at_cut)
    def _():
        greet((s, size - 1 - d))

    greet(far_side)
    for r in outward(rows_y)[:-1]:
        greet(y_peer(r))
    for r in range(1, Z_LO):
        greet((y * Z_LO + lax.rem(z_lo + r, Z_LO), d))
    for r in outward(half)[:-1]:
        greet((s, d - x_core + lax.rem(x_core + r, half)))

    data = pl.ds(PAD, ROWS)
    own = pl.ds(HALO, PLANES)
    loads = [
        pltpu.make_async_copy(fcur, u.at[1, :, own, data, :], local_sem.at[0]),
        pltpu.make_async_copy(fprev, u.at[0, :, own, data, :], local_sem.at[1]),
        pltpu.make_async_copy(c_in, cs.at[pl.ds(2, PLANES)], local_sem.at[2]),
        pltpu.make_async_copy(acur, stage_cur, local_sem.at[3]),
        pltpu.make_async_copy(anext, stage_next, local_sem.at[4]),
        pltpu.make_async_copy(observed_in, observed, local_sem.at[5]),
        pltpu.make_async_copy(rec_in, rec, local_sem.at[6]),
        pltpu.make_async_copy(moment_in, moment, local_sem.at[7]),
    ]
    for copy in loads:
        copy.start()

    pl.semaphore_wait(barrier, rows_y + Z_LO + half - 2 + jnp.where(at_cut, 1, 0))

    def copy_to(source, landing, send, recv, target):
        return pltpu.make_async_remote_copy(
            source, landing, send, recv, device_id=target, device_id_type=MESH
        )

    def first_copy(shot, side, target):
        return copy_to(
            fcur.at[shot, pl.ds((PLANES - 2) * side, 2)],
            u.at[1, shot, pl.ds(HALO - 2 + (PLANES + 2) * (1 - side), 2), data, :],
            init_send.at[shot, side], init_recv.at[shot, 1 - side], target,
        )

    def parcel(i, side):
        other = 1 - side
        if i == 0:
            return c_in.at[pl.ds((PLANES - 2) * side, 2)], cs.at[pl.ds((PLANES + 2) * other, 2)], relay.at[pl.ds(0, 2)]
        level, shot = (9, i - 1) if i < 3 else (8, i - 3)
        width = 2 if i < 3 else 4
        return (
            p.at[level, shot, pl.ds(HALO + (PLANES - width) * side, width), data, :],
            p.at[level, shot, pl.ds(HALO - width + (PLANES + width) * other, width), data, :],
            relay.at[pl.ds(2 * i if i < 3 else 4 * i - 6, width)],
        )

    def parcel_copy(i, side, target):
        source, landing, _ = parcel(i, side)
        return copy_to(source, landing, parcel_send.at[i, side], parcel_recv.at[i, 1 - side], target)

    relay_id = (s, jnp.where(d < half, 0, size - 1))
    relays = (d == 0) | (d == size - 1)

    def parcel_to_relay(i, side):
        source, _, middle = parcel(i, side)
        return copy_to(source, middle, parcel_send.at[i, side], relay_recv.at[i], relay_id)

    def parcel_from_relay(i, side):
        _, landing, middle = parcel(i, side)
        return copy_to(middle, landing, relay_send.at[i], parcel_recv.at[i, 1 - side], far_side)

    def post(items):
        for i in items:
            @pl.when(at_cut)
            def _():
                parcel_to_relay(i, late_side).start()

            @pl.when(has_late & jnp.logical_not(at_cut))
            def _():
                parcel_copy(i, late_side, late_id).start()

        for i in items:
            parcel_copy(i, early_side, early_id).start()

    def when_late(action):
        pl.when(has_late)(action)

    def halo_copy(buf, level, slot, shot, side, width, target):
        other = 1 - side
        return pltpu.make_async_remote_copy(
            buf.at[level, shot, pl.ds(HALO + (PLANES - width) * side, width), data, :],
            buf.at[level, shot, pl.ds(HALO - width + (PLANES + width) * other, width), data, :],
            send_sem.at[slot, shot, side],
            recv_sem.at[slot, shot, other],
            device_id=target,
            device_id_type=MESH,
        )

    for shot in range(SHOTS):
        when_late(lambda: first_copy(shot, late_side, late_id).start())
    for shot in range(SHOTS):
        first_copy(shot, early_side, early_id).start()
    post((0,))

    def pass_on(device):
        pl.semaphore_signal(token, inc=1, device_id=device, device_id_type=MESH)

    for r in outward(rows_y)[:-1]:
        pass_on(y_peer(r))
    pass_on(far_side)

    loads[2].wait()
    loads[3].wait()
    loads[4].wait()

    def scale(i, carry):
        factor = cs[2 + i]
        for shot in range(SHOTS):
            p[9, shot, HALO + i, PAD : PAD + ROWS, :] = factor * stage_next[shot, i]
            p[8, shot, HALO + i, PAD : PAD + ROWS, :] = factor * stage_cur[shot, i]
        return carry

    lax.fori_loop(0, PLANES, scale, 0)

    post(range(1, 5))

    def clear_pads(i, carry):
        level, plane = i // (PLANES + 2 * HALO), lax.rem(i, PLANES + 2 * HALO)
        zeros = jnp.zeros((PAD, LANES), jnp.float32)
        for buf in (u, p):
            for shot in range(SHOTS):
                buf[level, shot, plane, 0:PAD, :] = zeros
                buf[level, shot, plane, PAD + ROWS : 2 * PAD + ROWS, :] = zeros
        return carry

    lax.fori_loop(0, 10 * (PLANES + 2 * HALO), clear_pads, 0)

    @pl.when(jnp.logical_not(has_late))
    def _():
        first = (PLANES + HALO) * late_side

        def clear(i, carry):
            level, plane = i // HALO, first + lax.rem(i, HALO)
            zeros = jnp.zeros((ROWS, LANES), jnp.float32)
            for buf in (u, p):
                for shot in range(SHOTS):
                    buf[level, shot, plane, PAD : PAD + ROWS, :] = zeros
            return carry

        lax.fori_loop(0, 10 * HALO, clear, 0)
        for i in range(2):
            cs[(PLANES + 2) * late_side + i] = jnp.zeros((ROWS, LANES), jnp.float32)

    grad[...] = jnp.zeros_like(grad)

    for k in range(STEPS):
        cycle = lax.rem(ckpt[0] + k, 48).astype(jnp.float32)
        a = (jnp.full((1, LANES), cycle, jnp.float32) - 24.0) / 12.0
        wave[k : k + 1, :] = AMPLITUDE * (1.0 - 2.0 * a * a) * jnp.exp(-a * a)

    first_cell = (d * PLANES - 2) * (ROWS * LANES)
    rows_ext = EXT * ROWS
    row_at = lax.broadcasted_iota(jnp.int32, (rows_ext, NREC), 0)
    lane_at = lax.broadcasted_iota(jnp.int32, (LANES, NREC), 0)
    nt = (((1,), (1,)), ((), ()))

    def place(shot, carry):
        cell = rec[pl.ds(shot, 1), :] - first_cell
        row = lax.shift_right_arithmetic(cell, 7)
        lane = lax.bitwise_and(cell, 127)
        at_row = jnp.where(row_at == row, 1.0, 0.0).astype(jnp.bfloat16)
        lane_hit = lane_at == lane

        def put(values):
            right = jnp.where(lane_hit, values, 0.0).astype(jnp.bfloat16)
            return lax.dot_general(at_row, right, nt, preferred_element_type=jnp.float32)

        cnt[shot] = put(jnp.ones((1, NREC), jnp.float32)).reshape(EXT, ROWS, LANES)
        for k in range(STEPS):
            trace = observed[shot, k : k + 1, :]
            high = trace.astype(jnp.bfloat16).astype(jnp.float32)
            total = put(high) + put(trace - high)
            obs[k, shot] = total.reshape(EXT, ROWS, LANES)
        return carry

    cell_at = lax.broadcasted_iota(jnp.int32, (ROWS, LANES), 0) * LANES + lax.broadcasted_iota(jnp.int32, (ROWS, LANES), 1)
    for shot in range(SHOTS):
        source = src[shot] - first_cell
        for plane in range(EXT):
            hot[shot, plane] = jnp.where(cell_at == source - plane * (ROWS * LANES), 1.0, 0.0)

    lane_iota = lax.broadcasted_iota(jnp.int32, (ROWS, LANES), 1)
    masks = {j: (lane_iota >= j) if j > 0 else (lane_iota < LANES + j) for j in (1, 2, -1, -2)}

    def laplaces(buf, level, shot, start, count):
        def at(plane, dx):
            return buf[level, shot, start + plane, PAD + dx : PAD + dx + ROWS, :]

        def along_y(value, j):
            return jnp.where(masks[j], pltpu.roll(value, j % LANES, 1), 0.0)

        planes = {i: at(i, 0) for i in range(-2, count + 2)}
        out = []
        for i in range(count):
            center = planes[i]
            near = (planes[i - 1] + planes[i + 1]) + (at(i, -1) + at(i, 1)) + (along_y(center, 1) + along_y(center, -1))
            far = (planes[i - 2] + planes[i + 2]) + (at(i, -2) + at(i, 2)) + (along_y(center, 2) + along_y(center, -2))
            out.append((center, 3.0 * CENTER * center + NEAR * near + FAR * far))
        return out

    def forward(k, shot, start, count):
        strength = wave[pl.ds(k, 1), :]
        done = []
        for i, (center, value) in enumerate(laplaces(u, k + 1, shot, start, count)):
            plane = start + i
            value = value + strength * hot[shot, plane - 2]
            older = u[k, shot, plane, PAD : PAD + ROWS, :]
            done.append((plane, value, 2.0 * center - older + cs[plane - 2] * value))
        for plane, value, newer in done:
            lap[k, shot, plane - 2] = value
            u[k + 2, shot, plane, PAD : PAD + ROWS, :] = newer

    def backward(k, shot, start, count):
        done = []
        for i, (center, value) in enumerate(laplaces(p, k + 1, shot, start, count)):
            plane = start + i
            ahead = u[k + 2, shot, plane, PAD : PAD + ROWS, :]
            value = value + (cnt[shot, plane - 2] * ahead - obs[k, shot, plane - 2])
            later = p[k + 2, shot, plane, PAD : PAD + ROWS, :]
            newer = 2.0 * center - later + cs[plane - 2] * value
            done.append((plane, newer, grad[plane - 2] + newer * lap[k, shot, plane - 2]))
        for plane, newer, term in done:
            p[k, shot, plane, PAD : PAD + ROWS, :] = newer
            grad[plane - 2] = term

    even = 1 - odd
    loads[0].wait()
    loads[1].wait()

    def arrived(buf, level, slot, shot, side, width, target):
        halo_copy(buf, level, slot, shot, 1 - side, width, target).wait_recv()

    @pl.when(relays)
    def _():
        for i in range(5):
            parcel_to_relay(i, early_side).wait_recv()
            parcel_from_relay(i, early_side).start()

    for shot in range(SHOTS):
        first_copy(shot, 1 - early_side, early_id).wait_recv()
        forward(0, shot, 4 + 2 * even, 6)
        halo_copy(u, 2, 0, shot, early_side, 4, early_id).start()
    for shot in range(SHOTS):
        when_late(lambda: first_copy(shot, 1 - late_side, late_id).wait_recv())
        forward(0, shot, 4 + 6 * odd, 2)
        when_late(lambda: halo_copy(u, 2, 0, shot, late_side, 4, late_id).start())

    for load in loads[5:]:
        load.wait()
    lax.fori_loop(0, SHOTS, place, 0)

    parcel_copy(0, 1 - early_side, early_id).wait_recv()
    when_late(lambda: parcel_copy(0, 1 - late_side, late_id).wait_recv())

    def forward_round(j, carry):
        k = 2 * j + 1

        def leave(shot, side, target):
            @pl.when(j < 3)
            def _():
                halo_copy(u, k + 3, j + 1, shot, side, 4, target).start()

        def second(shot, start):
            @pl.when(j < 3)
            def _():
                forward(k + 1, shot, start, 4)

        for shot in range(SHOTS):
            arrived(u, k + 1, j, shot, early_side, 4, early_id)
            forward(k, shot, 2 + 4 * even, 8)
            second(shot, 4 + 4 * even)
            leave(shot, early_side, early_id)
        for shot in range(SHOTS):
            when_late(lambda: arrived(u, k + 1, j, shot, late_side, 4, late_id))
            forward(k, shot, 2 + 8 * odd, 4)
            second(shot, 4 + 4 * odd)
            when_late(lambda: leave(shot, late_side, late_id))
        return carry

    lax.fori_loop(0, 4, forward_round, 0)

    for i in range(1, 5):
        parcel_copy(i, 1 - early_side, early_id).wait_recv()
        when_late(lambda: parcel_copy(i, 1 - late_side, late_id).wait_recv())

    per_plane = shots // PLANES
    block_rows = ROWS // per_plane
    cells_all = size * PLANES * ROWS * LANES

    def remote(source, target, sem, device):
        return pltpu.make_async_remote_copy(
            source, target, all_send.at[sem], all_recv.at[sem], device_id=device, device_id_type=MESH
        )

    def scatter(side):
        first = (PLANES // 2) * side
        for i in range(PLANES // 2):
            blocks[pl.ds((first + i) * per_plane, per_plane)] = (grad[2 + first + i] / cs[2 + first + i]).reshape(
                per_plane, block_rows, LANES
            )

    pl.semaphore_wait(token, rows_y)

    def backward_round(i, carry):
        k = 7 - 2 * i

        def arrive(shot, side, target):
            @pl.when(i > 0)
            def _():
                arrived(p, k + 1, 3 + i, shot, side, 4, target)

        def leave(shot, side, target):
            @pl.when(i < 3)
            def _():
                halo_copy(p, k - 1, 4 + i, shot, side, 4, target).start()

        for shot in range(SHOTS):
            arrive(shot, early_side, early_id)
            backward(k, shot, 2 + 4 * even, 8)
            backward(k - 1, shot, 4 + 4 * even, 4)
            leave(shot, early_side, early_id)

        for shot in range(SHOTS):
            when_late(lambda: arrive(shot, late_side, late_id))
            backward(k, shot, 2 + 8 * odd, 4)
            backward(k - 1, shot, 4 + 4 * odd, 4)
            when_late(lambda: leave(shot, late_side, late_id))
        return carry

    lax.fori_loop(0, 4, backward_round, 0)

    scatter(late_side)
    scatter(early_side)

    def shot_peers():
        for dy in outward(rows_y):
            for dz in range(Z_LO):
                if dy or dz:
                    yield lax.rem(y + dy, rows_y) * Z_LO + lax.rem(z_lo + dz, Z_LO)

    others = pl.ds(0, shots - 1)
    plane = d * PLANES + s // per_plane
    weight = 1.0 + 2.0 * plane.astype(jnp.float32) / (size * PLANES - 1)
    off_cut = jnp.logical_not(at_cut)
    line = pl.ds(y * Z_LO, Z_LO)
    others_y, others_line = pl.ds(0, (rows_y - 1) * Z_LO), pl.ds(0, Z_LO - 1)

    def z_peers():
        for r in range(1, Z_LO):
            to = lax.rem(z_lo + r, Z_LO)
            yield to, (y * Z_LO + to, d)

    @pl.when(at_cut)
    def _():
        for j in shot_peers():
            remote(blocks.at[j], parts.at[s], 0, (j, d)).start()
        parts[s] = blocks[s]
        remote(parts.at[others], parts.at[others], 0, (s, d)).wait_recv()
        scaled[s] = weight * lax.fori_loop(1, shots, lambda j, t: t + parts[j], parts[0])

    @pl.when(off_cut)
    def _():
        for r in outward(rows_y)[:-1]:
            to = lax.rem(y + r, rows_y)
            remote(blocks.at[pl.ds(to * Z_LO, Z_LO)], parts.at[line], 4, y_peer(r)).start()
        parts[line] = blocks[line]
        remote(parts.at[others_y], parts.at[others_y], 4, (s, d)).wait_recv()
        lines[...] = lax.fori_loop(1, rows_y, lambda j, t: t + parts[pl.ds(j * Z_LO, Z_LO)], parts[0:Z_LO])
        for to, device in z_peers():
            remote(lines.at[to], line_parts.at[z_lo], 5, device).start()
        line_parts[z_lo] = lines[z_lo]
        remote(line_parts.at[others_line], line_parts.at[others_line], 5, (s, d)).wait_recv()
        scaled[s] = weight * lax.fori_loop(1, Z_LO, lambda j, t: t + line_parts[j], line_parts[0])

    mine = scaled[s]
    old = moment[s]
    squares = jnp.sum(mine * mine)

    column, plane_at = z * 2 + lax.rem(d, 2), y * chips_x + x
    for q, value in enumerate((squares, weight * jnp.sum(old * old), weight * jnp.sum(old * mine), weight * squares)):
        z_tiles[column, q : q + 1, :] = jnp.full((1, LANES), value, jnp.float32)
    z_tiles[column, 4:8, :] = jnp.zeros((4, LANES), jnp.float32)
    for dz in outward(chips_z):
        to_z = lax.rem(z + dz, chips_z)
        for flip in range(2):
            if dz or flip:
                core = lax.rem(d + flip, 2)
                device = (y * Z_LO + lax.rem(to_z, Z_LO), (to_z // Z_LO) * half + x * 2 + core)
                remote(z_tiles.at[column], z_tiles.at[column], 1, device).start()

    @pl.when(at_cut)
    def _():
        for j in shot_peers():
            remote(scaled.at[s], scaled.at[s], 2, (j, d)).start()

    @pl.when(off_cut)
    def _():
        for _, device in z_peers():
            remote(scaled.at[s], scaled.at[s], 6, device).start()
        remote(scaled.at[others_line], scaled.at[others_line], 6, (s, d)).wait_recv()
        for r in outward(rows_y)[:-1]:
            remote(scaled.at[line], scaled.at[line], 2, y_peer(r)).start()

    others_z, others_xy = pl.ds(0, 2 * chips_z - 1), pl.ds(0, rows_y * chips_x - 1)
    remote(z_tiles.at[others_z], z_tiles.at[others_z], 1, (s, d)).wait_recv()
    xy_tiles[plane_at] = lax.fori_loop(1, 2 * chips_z, lambda j, t: t + z_tiles[j], z_tiles[0])
    for dy in outward(rows_y):
        for dx in outward(chips_x):
            if dy or dx:
                device = (lax.rem(y + dy, rows_y) * Z_LO + z_lo, z_hi * half + lax.rem(x + dx, chips_x) * 2 + lax.rem(d, 2))
                remote(xy_tiles.at[plane_at], xy_tiles.at[plane_at], 3, device).start()

    def sent(side, target):
        for i in range(5):
            parcel_copy(i, side, target).wait_send()
        for shot in range(SHOTS):
            first_copy(shot, side, target).wait_send()
            for slot, buf, level in ((0, u, 2), (1, u, 4), (2, u, 6), (3, u, 8), (4, p, 6), (5, p, 4), (6, p, 2)):
                halo_copy(buf, level, slot, shot, side, 4, target).wait_send()

    sent(early_side, early_id)
    when_late(lambda: sent(late_side, late_id))

    @pl.when(relays)
    def _():
        for i in range(5):
            parcel_from_relay(i, early_side).wait_send()

    @pl.when(at_cut)
    def _():
        remote(parts.at[others], parts.at[others], 0, (s, d)).wait_send()
        remote(scaled.at[others], scaled.at[others], 2, (s, d)).wait_send()

    @pl.when(off_cut)
    def _():
        remote(parts.at[others_y], parts.at[others_y], 4, (s, d)).wait_send()
        remote(line_parts.at[others_line], line_parts.at[others_line], 5, (s, d)).wait_send()
        remote(scaled.at[others_line], scaled.at[others_line], 6, (s, d)).wait_send()
        remote(scaled.at[others_y], scaled.at[others_y], 2, (s, d)).wait_send()

    remote(z_tiles.at[others_z], z_tiles.at[others_z], 1, (s, d)).wait_send()
    remote(xy_tiles.at[others_xy], xy_tiles.at[others_xy], 3, (s, d)).wait_send()
    remote(xy_tiles.at[others_xy], xy_tiles.at[others_xy], 3, (s, d)).wait_recv()
    grand = lax.fori_loop(1, rows_y * chips_x, lambda j, t: t + xy_tiles[j], xy_tiles[0])
    step = 0.5 * lax.rsqrt(grand[0:1, :] / cells_all + EPSILON)
    energy = grand[1:2, :] - 2.0 * step * grand[2:3, :] + step * step * grand[3:4, :]
    kinetic_out[...] = 0.5 * energy / cells_all

    @pl.when(at_cut)
    def _():
        remote(scaled.at[others], scaled.at[others], 2, (s, d)).wait_recv()

    @pl.when(off_cut)
    def _():
        remote(scaled.at[others_y], scaled.at[others_y], 2, (s, d)).wait_recv()

    def update(j, carry):
        half_out[j] = moment[j] - step * scaled[j]
        return carry

    lax.fori_loop(0, shots, update, 0)


def window(c, momentum, fprev, fcur, anext, acur, observed, src, rec, ckpt, ns, nd):
    any_space = pl.BlockSpec(memory_space=pl.ANY)
    in_vmem = pl.BlockSpec(memory_space=pltpu.VMEM)
    in_smem = pl.BlockSpec(memory_space=pltpu.SMEM)
    padded = (10, SHOTS, PLANES + 2 * HALO, ROWS + 2 * PAD, LANES)
    f32 = jnp.float32
    blocks = (ns, PLANES * ROWS // ns, LANES)
    half, kinetic = pl.pallas_call(
        window_kernel,
        out_shape=(jax.ShapeDtypeStruct(blocks, f32), jax.ShapeDtypeStruct((1, LANES), f32)),
        in_specs=[any_space] * 6 + [in_smem, any_space, in_smem, any_space],
        out_specs=(in_vmem, in_vmem),
        scratch_shapes=[
            pltpu.VMEM(padded, f32),
            pltpu.VMEM(padded, f32),
            pltpu.VMEM((STEPS, SHOTS, EXT, ROWS, LANES), f32),
            pltpu.VMEM((STEPS, SHOTS, EXT, ROWS, LANES), f32),
            pltpu.VMEM((SHOTS, EXT, ROWS, LANES), f32),
            pltpu.VMEM((SHOTS, EXT, ROWS, LANES), f32),
            pltpu.VMEM((EXT, ROWS, LANES), f32),
            pltpu.VMEM((EXT, ROWS, LANES), f32),
            pltpu.VMEM((STEPS, LANES), f32),
            pltpu.VMEM((SHOTS, PLANES, ROWS, LANES), f32),
            pltpu.VMEM((SHOTS, PLANES, ROWS, LANES), f32),
            pltpu.VMEM(blocks, f32),
            pltpu.VMEM(blocks, f32),
            pltpu.VMEM(blocks, f32),
            pltpu.VMEM((4 * Z_LO, 8, LANES), f32),
            pltpu.VMEM((ns // Z_LO * nd // 4, 8, LANES), f32),
            pltpu.VMEM((14, ROWS, LANES), f32),
            pltpu.VMEM((SHOTS, STEPS, NREC), f32),
            pltpu.VMEM((SHOTS, NREC), jnp.int32),
            pltpu.VMEM(blocks, f32),
            pltpu.VMEM((Z_LO,) + blocks[1:], f32),
            pltpu.VMEM((Z_LO,) + blocks[1:], f32),
            pltpu.SemaphoreType.DMA((8,)),
            pltpu.SemaphoreType.DMA((7, SHOTS, 2)),
            pltpu.SemaphoreType.DMA((7, SHOTS, 2)),
            pltpu.SemaphoreType.DMA((SHOTS, 2)),
            pltpu.SemaphoreType.DMA((SHOTS, 2)),
            pltpu.SemaphoreType.DMA((5, 2)),
            pltpu.SemaphoreType.DMA((5, 2)),
            pltpu.SemaphoreType.DMA((5,)),
            pltpu.SemaphoreType.DMA((5,)),
            pltpu.SemaphoreType.DMA((7,)),
            pltpu.SemaphoreType.DMA((7,)),
            pltpu.SemaphoreType.REGULAR,
        ],
        compiler_params=pltpu.CompilerParams(
            collective_id=0, has_side_effects=True, vmem_limit_bytes=60 * 1024 * 1024
        ),
        name="window",
    )(c, fprev, fcur, anext, acur, observed, src, rec, ckpt, momentum.reshape(blocks))
    return half.reshape(momentum.shape), kinetic[0, 0]


def solution(mesh):
    def shards(c, momentum, fprev, fcur, anext, acur, observed, src, rec, ckpt):
        return window(
            c, momentum, fprev, fcur, anext, acur, observed, src, rec, ckpt.reshape(1),
            mesh.shape["shot"], mesh.shape["depth"],
        )

    placed = (
        P("depth", None, None),
        P("depth", None, None),
        P("shot", "depth", None, None),
        P("shot", "depth", None, None),
        P("shot", "depth", None, None),
        P("shot", "depth", None, None),
        P("shot", None, None),
        P("shot"),
        P("shot", None),
        P(),
    )
    return jax.shard_map(
        shards, mesh=mesh, in_specs=placed, out_specs=(P("depth", None, None), P()), check_vma=False
    )
```
